128 devices in a mesh: req: 16 (over y_hi, z, core), tp: 8 (over y_lo, x).
Axes of the slice: x: 4, y: 4 (y_hi: 2, y_lo: 2; y = y_hi * 2 + y_lo), z: 4, core: 2. Of those that a mesh axis runs over, the one named last changes fastest.
Arguments:
- query: bfloat16 [512, 6, 64, 128], P('req', None, 'tp'), may hold values from -14 to 14
- k_cache: bfloat16 [512, 8, 1024, 128], P('req', 'tp'), may hold values from -14 to 14
- v_cache: bfloat16 [512, 8, 1024, 128], P('req', 'tp'), may hold values from -6 to 6
- ctx_len: int32 [512], P('req'), may hold values from 8 to 1024, as said below
- residual: bfloat16 [3072, 8192], P('req', 'tp'), may hold values from -2.5 to 2.5
- accepted: int32 [512], replicated, may hold values from 0 to 5, as said below
- w_draft: bfloat16 [8192, 8, 1024], P('tp', None, 'req'), may hold values from -0.0625 to 0.0625
Outputs:
- hidden: bfloat16 [3072, 8192], P('req', 'tp')
- grad_w: float32 [8192, 8, 1024], P('tp', None, 'req')
The draws below stay inside these ranges and needn't reach their ends.
Inputs may be any that keep to these rules, and one draw needn't show every extreme that they name: `ctx_len`: A request's live slots end with its 6 verified positions; some request has 1024. `accepted`: the counts of each aligned block of 32 requests sum to exactly 80.
All inputs are finite; a program needn't handle non-finite values.
Results may differ from the reference program's by a relative error of at most 0.015.
Values may be sent and summed in bfloat16 or wider, within the bound.
A program may use at most 128 MiB of HBM per device.

```python
import jax
import jax.numpy as jnp
from jax import lax

D = 8192
H = 64
KVH = 8
HD = 128
QLEN = 6
CTX = 1024
REQ_DEV = 32
GW = 1024
REQS = 512
ROWS = 3072
N_TP = 8


def draw_k_cache(key, part):
    key = jax.random.fold_in(key, 1)
    values = jnp.clip(jax.random.normal(key, (REQS, KVH, CTX, HD), jnp.float32), -4.0, 4.0)
    return values.astype(jnp.bfloat16)


def draw_query(key, part):
    key = jax.random.fold_in(key, 2)
    values = jnp.clip(jax.random.normal(key, (REQS, QLEN, H, HD), jnp.float32), -4.0, 4.0)
    return values.astype(jnp.bfloat16)


def draw_ctx_len(key, part):
    key = jax.random.fold_in(key, 3)
    short = jax.random.randint(key, (REQS,), QLEN + 2, CTX // 4 + 1)
    longer = jax.random.randint(jax.random.fold_in(key, 4), (REQS,), QLEN + 2, CTX + 1)
    pick = jax.random.randint(jax.random.fold_in(key, 6), (REQS,), 0, 64) == 0
    lengths = jnp.where(pick, longer, short)
    spot = jax.random.randint(jax.random.fold_in(key, 5), (), 0, REQS)
    lengths = lengths.at[spot].set(CTX)
    return lengths.astype(jnp.int32)


def draw_accepted(key, part):
    key = jax.random.fold_in(key, 8)
    blocks = REQS // REQ_DEV
    half = REQ_DEV // 2
    first = jax.random.randint(key, (blocks, half), 0, QLEN)
    first = first.at[0, 0].set(0)
    paired = jnp.concatenate([first, QLEN - 1 - first], axis=1)
    scores = jax.random.randint(jax.random.fold_in(key, 9), (blocks, REQ_DEV), 0, 1 << 20)
    scores = scores * REQ_DEV + jnp.arange(REQ_DEV)[None, :]
    order = jnp.argsort(scores, axis=1)
    mixed = jnp.take_along_axis(paired, order, axis=1)
    return mixed.reshape(REQS).astype(jnp.int32)


def block_scale(own_key, extent, split, smallest, top_value):
    def one(dim, shards_of):
        steps = jax.random.uniform(jax.random.fold_in(jax.random.fold_in(own_key, 6), dim), (shards_of,), jnp.float32, smallest / len(split), top_value / len(split))
        return jnp.repeat(jnp.exp(steps), extent[dim] // shards_of).reshape((-1,) + (1,) * (len(extent) - dim - 1))

    gain = one(*split[0])
    for cut in split[1:]:
        gain = gain * one(*cut)
    return gain


def centred(rng, shape, deviation, bound, cuts=(), held_as=jnp.bfloat16):
    entries = jax.random.normal(rng, shape, jnp.float32) * deviation
    if len(cuts) > 0:
        entries = block_scale(rng, shape, cuts, -0.22, 0.18) * entries
    return jnp.clip(entries, min=-bound, max=bound).astype(held_as)


def setup_inputs(seed: int = 0) -> dict:
    streams_of = jax.random.split(jax.random.key(seed), 8)
    query = draw_query(jax.random.fold_in(streams_of[7], 71), 0)
    k_cache = draw_k_cache(jax.random.fold_in(streams_of[7], 71), 0)
    v_cache = centred(streams_of[2], (REQS, KVH, CTX, HD), 1.0, 6.0, ((0, 16), (1, 8)))
    ctx_len = draw_ctx_len(jax.random.fold_in(streams_of[7], 71), 0)
    residual = centred(streams_of[4], (ROWS, D), 0.3, 2.5, ((0, 16), (1, 8)))
    accepted = draw_accepted(jax.random.fold_in(streams_of[7], 71), 0)
    w_draft = centred(streams_of[6], (D, KVH, GW), D ** -0.5, 0.0625, ((0, 8), (2, 16)))
    return {"query": query, "k_cache": k_cache, "v_cache": v_cache, "ctx_len": ctx_len, "residual": residual, "accepted": accepted, "w_draft": w_draft}


def reference(query, k_cache, v_cache, ctx_len, residual, accepted, w_draft):
    group = H // KVH

    def one_request(items):
        queries, keys, values, length = items
        grouped = queries.astype(jnp.float32).reshape(QLEN, KVH, group, HD).transpose(1, 2, 0, 3)
        scores = jnp.einsum("kgqd,ktd->kgqt", grouped, keys.astype(jnp.float32)) * (HD ** -0.5)
        limit = length - QLEN + jnp.arange(QLEN, dtype=jnp.int32) + 1
        allowed = jnp.arange(CTX, dtype=jnp.int32)[None, :] < limit[:, None]
        scores = jnp.where(allowed[None, None], scores, -jnp.inf)
        top = jnp.max(scores, axis=-1, keepdims=True)
        rounded = lax.optimization_barrier(jnp.exp(scores - top).astype(jnp.bfloat16))
        weights = rounded.astype(jnp.float32)
        total = jnp.sum(weights, axis=-1, keepdims=True)
        mixed = jnp.einsum("kgqt,ktd->kgqd", weights, values.astype(jnp.float32)) / total
        return mixed.transpose(2, 0, 1, 3).reshape(QLEN, D)

    attention = lax.map(one_request, (query, k_cache, v_cache, ctx_len)).reshape(ROWS, D)
    hidden = (residual.astype(jnp.float32) + attention).astype(jnp.bfloat16)
    block = D // N_TP
    blocks_rows = hidden.reshape(ROWS, N_TP, block).transpose(1, 0, 2)
    blocks_weight = w_draft.reshape(N_TP, block, D)

    def add_block(total, pair):
        rows_part, weight_part = pair
        product = jnp.dot(rows_part, weight_part, preferred_element_type=jnp.float32)
        rounded = lax.optimization_barrier(product.astype(jnp.bfloat16))
        return total + rounded.astype(jnp.float32), None

    draft, _ = lax.scan(add_block, jnp.zeros((ROWS, D), jnp.float32), (blocks_rows, blocks_weight))
    shaped = hidden.reshape(REQS, QLEN, D)
    following = jnp.concatenate([shaped[:, 1:], jnp.zeros_like(shaped[:, :1])], axis=1).reshape(ROWS, D)
    used = (jnp.arange(QLEN, dtype=jnp.int32)[None, :] < accepted[:, None]).astype(jnp.float32).reshape(ROWS, 1)
    residual_grad = (used * (draft - following.astype(jnp.float32)) / QLEN).astype(jnp.bfloat16)
    grad_w = lax.dot_general(hidden, residual_grad, (((0,), (0,)), ((), ())), preferred_element_type=jnp.float32)
    return hidden, grad_w.reshape(D, KVH, GW)
```

```python
import functools

import jax
import jax.numpy as jnp
from jax import lax
from jax.experimental import pallas as pl
from jax.experimental.pallas import tpu as pltpu
from jax.sharding import PartitionSpec as P

QLEN = 6
GROUP = 8
USED_PER_BLOCK = 80
SHORT = 256
BATCH = 4

MESH = pl.DeviceIdType.MESH


def attend(queries, keys, values, length, scale):
    slots = keys.shape[0]
    scores = (
        lax.dot_general(
            queries, keys, (((1,), (1,)), ((), ())), preferred_element_type=jnp.float32
        )
        * scale
    )
    rows = queries.shape[0]
    position = lax.broadcasted_iota(jnp.int32, (rows, slots), 1)
    verified = lax.broadcasted_iota(jnp.int32, (rows, slots), 0) // GROUP
    scores = jnp.where(position < verified + (length - QLEN + 1), scores, -jnp.inf)
    top = jnp.max(scores, axis=-1, keepdims=True)
    weights = jnp.exp(scores - top).astype(jnp.bfloat16)
    total = jnp.sum(weights.astype(jnp.float32), axis=-1, keepdims=True)
    mixed = jnp.dot(weights, values, preferred_element_type=jnp.float32)
    return mixed / total


def attention_kernel(
    ctx_ref, accepted_ref, q_hbm, k_hbm, v_hbm, res_hbm,
    hidden_hbm, used_ref, foll_ref,
    q_buf, k_buf, v_buf, res_buf, att_buf, hid_buf, k_sem, v_sem, k_more, v_more, io_sem,
):
    requests, slots, head_dim = k_hbm.shape
    rows = q_buf.shape[1]
    scale = head_dim ** (-0.5)
    batches = requests // BATCH
    q_copy = pltpu.make_async_copy(q_hbm, q_buf, io_sem.at[0])
    res_copy = pltpu.make_async_copy(res_hbm, res_buf, io_sem.at[1])
    q_copy.start()

    def short_copies(b):
        span = (pl.ds(b * BATCH, BATCH), pl.ds(0, SHORT))
        return (
            pltpu.make_async_copy(k_hbm.at[span], k_buf.at[span], k_sem.at[b]),
            pltpu.make_async_copy(v_hbm.at[span], v_buf.at[span], v_sem.at[b]),
        )

    def more_copies(r):
        span = (r, pl.ds(SHORT, slots - SHORT))
        return (
            pltpu.make_async_copy(k_hbm.at[span], k_buf.at[span], k_more.at[r]),
            pltpu.make_async_copy(v_hbm.at[span], v_buf.at[span], v_more.at[r]),
        )

    for b in range(batches):
        for copy in short_copies(b):
            copy.start()
    res_copy.start()

    @pl.loop(0, requests)
    def _(r):
        @pl.when(ctx_ref[r] > SHORT)
        def _():
            for copy in more_copies(r):
                copy.start()

    q_copy.wait()

    @pl.loop(0, batches)
    def _(b):
        for copy in short_copies(b):
            copy.wait()
        for j in range(BATCH):
            r = b * BATCH + j
            att_buf[pl.ds(pl.multiple_of(r * rows, rows), rows), :] = attend(
                q_buf[r], k_buf[r, 0:SHORT], v_buf[r, 0:SHORT], ctx_ref[r], scale
            )

    @pl.loop(0, requests)
    def _(r):
        @pl.when(ctx_ref[r] > SHORT)
        def _():
            for copy in more_copies(r):
                copy.wait()
            att_buf[pl.ds(pl.multiple_of(r * rows, rows), rows), :] = attend(
                q_buf[r], k_buf[r], v_buf[r], ctx_ref[r], scale
            )

    res_copy.wait()
    all_rows = requests * QLEN
    for h in range(GROUP):
        columns = pl.ds(h * head_dim, head_dim)
        mixed = att_buf[pl.ds(h, all_rows, stride=GROUP), :]
        hid_buf[:, columns] = (res_buf[:, columns].astype(jnp.float32) + mixed).astype(jnp.bfloat16)
    hidden_copy = pltpu.make_async_copy(hid_buf, hidden_hbm, io_sem.at[2])
    hidden_copy.start()

    row = lax.broadcasted_iota(jnp.int32, (1, all_rows), 1)
    request = row // QLEN
    verified = row - request * QLEN
    base = lax.axis_index("req") * requests
    place = jnp.full((1, all_rows), -1, jnp.int32)
    next_place = place
    before = jnp.int32(0)
    for r in range(requests):
        count = accepted_ref[base + r]
        mine = request == r
        place = jnp.where(mine & (verified < count), before + verified, place)
        next_place = jnp.where(
            mine & (verified >= 1) & (verified <= count), before + verified - 1, next_place
        )
        before = before + count
    hidden = hid_buf[...]
    want = lax.broadcasted_iota(jnp.int32, (used_ref.shape[0], all_rows), 0)
    pick = (want == place).astype(jnp.float32).astype(jnp.bfloat16)
    used_ref[...] = jnp.dot(pick, hidden, preferred_element_type=jnp.float32).astype(jnp.bfloat16)
    want = lax.broadcasted_iota(jnp.int32, (foll_ref.shape[1], all_rows), 0)
    pick = (want == next_place).astype(jnp.float32).astype(jnp.bfloat16)
    following = jnp.dot(pick, hidden, preferred_element_type=jnp.float32)
    foll_ref[...] = following.T.astype(jnp.bfloat16)
    hidden_copy.wait()


def attention(query, k_cache, v_cache, ctx_len, residual, accepted):
    requests, slots, head_dim = k_cache.shape
    rows = query.shape[1]
    all_rows, features = residual.shape
    any_spec = pl.BlockSpec(memory_space=pl.ANY)
    smem = pl.BlockSpec(memory_space=pltpu.SMEM)
    vmem = pl.BlockSpec(memory_space=pltpu.VMEM)
    batches = requests // BATCH
    return pl.pallas_call(
        attention_kernel,
        out_shape=(
            jax.ShapeDtypeStruct((all_rows, features), jnp.bfloat16),
            jax.ShapeDtypeStruct((USED_PER_BLOCK, features), jnp.bfloat16),
            jax.ShapeDtypeStruct((features, 128), jnp.bfloat16),
        ),
        in_specs=[smem, smem, any_spec, any_spec, any_spec, any_spec],
        out_specs=(any_spec, vmem, vmem),
        scratch_shapes=[
            pltpu.VMEM((requests, rows, head_dim), jnp.bfloat16),
            pltpu.VMEM((requests, slots, head_dim), jnp.bfloat16),
            pltpu.VMEM((requests, slots, head_dim), jnp.bfloat16),
            pltpu.VMEM((all_rows, features), jnp.bfloat16),
            pltpu.VMEM((requests * rows, head_dim), jnp.float32),
            pltpu.VMEM((all_rows, features), jnp.bfloat16),
            pltpu.SemaphoreType.DMA((batches,)),
            pltpu.SemaphoreType.DMA((batches,)),
            pltpu.SemaphoreType.DMA((requests,)),
            pltpu.SemaphoreType.DMA((requests,)),
            pltpu.SemaphoreType.DMA((3,)),
        ],
        compiler_params=pltpu.CompilerParams(vmem_limit_bytes=40 * 2**20),
        name="attention",
    )(ctx_len, accepted, query, k_cache, v_cache, residual)


OFFSETS = ((0, 0), (0, 1), (0, 3), (0, 2), (1, 0), (1, 1), (1, 3), (1, 2))


def gradient_kernel(
    n_tp, used_ref, foll_ref, w_ref, out_ref,
    hid, w_buf, foll, place, part, sums, grad, total,
    io_sem, ag_send, ag_recv, sib_send, sib_recv, fo_send, fo_recv,
    rs_send, rs_recv, gg_send, gg_recv,
):
    r = lax.axis_index("req")
    t = lax.axis_index("tp")
    core = lax.rem(r, 2)
    z = lax.rem(r // 2, 4)
    y_hi = r // 8
    sibling = r + 1 - 2 * core
    n_req = 16
    block = used_ref.shape[0]
    width = foll.shape[1]
    chunk = part.shape[2]

    def rows_of(source):
        return pl.ds(pl.multiple_of(source * block, block), block)

    w_copy = pltpu.make_async_copy(w_ref, w_buf, io_sem.at[0])
    own_copy = pltpu.make_async_copy(used_ref, hid.at[rows_of(r)], io_sem.at[1])
    foll_copy = pltpu.make_async_copy(
        foll_ref.at[pl.ds(pl.multiple_of(r * width, width), width)], foll.at[r], io_sem.at[2]
    )
    w_copy.start()
    own_copy.start()
    foll_copy.start()

    barrier = pltpu.get_barrier_semaphore()

    @pl.loop(1, n_req)
    def _(i):
        pl.semaphore_signal(
            barrier, inc=1, device_id={"req": lax.rem(r + i, n_req)}, device_id_type=MESH
        )

    @pl.loop(1, n_tp)
    def _(i):
        pl.semaphore_signal(
            barrier, inc=1, device_id={"tp": lax.rem(t + i, n_tp)}, device_id_type=MESH
        )

    pl.semaphore_wait(barrier, n_req - 1 + n_tp - 1)

    def peer(k, sign):
        dy, dz = OFFSETS[k]
        return (lax.rem(y_hi + dy, 2) * 4 + lax.rem(z + 4 + sign * dz, 4)) * 2 + core

    def gather_copy(k):
        return pltpu.make_async_remote_copy(
            src_ref=used_ref, dst_ref=hid.at[rows_of(r)],
            send_sem=ag_send.at[k], recv_sem=ag_recv.at[k],
            device_id={"req": peer(k, 1)}, device_id_type=MESH,
        )

    def sibling_copy(k):
        source = peer(k, -1)
        return pltpu.make_async_remote_copy(
            src_ref=used_ref if k == 0 else hid.at[rows_of(source)],
            dst_ref=hid.at[rows_of(source)],
            send_sem=sib_send.at[k], recv_sem=sib_recv.at[k],
            device_id={"req": sibling}, device_id_type=MESH,
        )

    def gather_wait(k):
        pltpu.make_async_remote_copy(
            src_ref=used_ref, dst_ref=hid.at[rows_of(peer(k, -1))],
            send_sem=ag_send.at[k], recv_sem=ag_recv.at[k],
            device_id={"req": peer(k, 1)}, device_id_type=MESH,
        ).wait_recv()

    def sibling_wait(k):
        source = peer(k, -1)
        other = source + 1 - 2 * core
        pltpu.make_async_remote_copy(
            src_ref=used_ref, dst_ref=hid.at[rows_of(other)],
            send_sem=sib_send.at[k], recv_sem=sib_recv.at[k],
            device_id={"req": sibling}, device_id_type=MESH,
        ).wait_recv()

    sibling_copy(0).start()
    for k in range(1, 8):
        gather_copy(k).start()

    def foll_exchange(i):
        target = lax.rem(r + i, n_req)
        return pltpu.make_async_remote_copy(
            src_ref=foll_ref.at[pl.ds(pl.multiple_of(target * width, width), width)],
            dst_ref=foll.at[r],
            send_sem=fo_send.at[i], recv_sem=fo_recv.at[i],
            device_id={"req": target}, device_id_type=MESH,
        )

    @pl.loop(1, n_req)
    def _(i):
        foll_exchange(i).start()

    @pl.loop(0, 8)
    def _(s):
        j = lax.broadcasted_iota(jnp.int32, (128, chunk), 0)
        column = lax.broadcasted_iota(jnp.int32, (128, chunk), 1)
        hit = (column == s * block + j) & (j < block)
        place[pl.ds(pl.multiple_of(s * 128, 128), 128), :] = hit.astype(jnp.float32).astype(
            jnp.bfloat16
        )

    own_copy.wait()
    w_copy.wait()

    def rs_copy(h, i):
        target = lax.rem(t + i, n_tp)
        return pltpu.make_async_remote_copy(
            src_ref=part.at[h, pl.ds(pl.multiple_of(target * width, width), width)],
            dst_ref=sums.at[h, i],
            send_sem=rs_send.at[h, i], recv_sem=rs_recv.at[h, i],
            device_id={"tp": target}, device_id_type=MESH,
        )

    def gg_copy(h, i):
        mine = pl.ds(pl.multiple_of(t * width, width), width)
        return pltpu.make_async_remote_copy(
            src_ref=grad.at[h, mine], dst_ref=grad.at[h, mine],
            send_sem=gg_send.at[h, i], recv_sem=gg_recv.at[h, i],
            device_id={"tp": lax.rem(t + i, n_tp)}, device_id_type=MESH,
        )

    def gg_wait(h, i):
        source = lax.rem(t + n_tp - i, n_tp)
        theirs = pl.ds(pl.multiple_of(source * width, width), width)
        pltpu.make_async_remote_copy(
            src_ref=grad.at[h, theirs], dst_ref=grad.at[h, theirs],
            send_sem=gg_send.at[h, i], recv_sem=gg_recv.at[h, i],
            device_id={"tp": lax.rem(t + i, n_tp)}, device_id_type=MESH,
        ).wait_recv()

    def chunk_start(h):
        return pl.multiple_of(lax.rem(y_hi + h, 2) * chunk, chunk)

    def draft(h):
        start = chunk_start(h)

        @pl.loop(0, chunk // 128)
        def _(n):
            rows = hid[pl.ds(pl.multiple_of(start + n * 128, 128), 128), :]
            part[h, :, pl.ds(pl.multiple_of(n * 128, 128), 128)] = lax.dot_general(
                w_buf[...], rows, (((1,), (1,)), ((), ())), preferred_element_type=jnp.float32
            ).astype(jnp.bfloat16)

        @pl.loop(1, n_tp)
        def _(i):
            rs_copy(h, i).start()

    def loss_grad(h):
        @pl.loop(1, n_tp)
        def _(i):
            rs_copy(h, i).wait_recv()

        mine = pl.ds(pl.multiple_of(t * width, width), width)
        summed = part[h, mine, :].astype(jnp.float32)
        for i in range(1, n_tp):
            summed = summed + sums[h, i].astype(jnp.float32)
        first = lax.rem(y_hi + h, 2) * 8
        rows = jnp.concatenate([foll[first + s] for s in range(8)], axis=1)
        following = jnp.dot(rows, place[...], preferred_element_type=jnp.float32)
        grad[h, mine, :] = ((summed - following) / QLEN).astype(jnp.bfloat16)

        @pl.loop(1, n_tp)
        def _(i):
            gg_copy(h, i).start()

    def project(h):
        @pl.loop(1, n_tp)
        def _(i):
            gg_wait(h, i)

        start = chunk_start(h)
        features = hid.shape[1]
        tile = min(256, features)

        @pl.loop(0, features // tile)
        def _(n):
            columns = pl.ds(pl.multiple_of(n * tile, tile), tile)
            value = jnp.dot(
                grad[h], hid[pl.ds(start, chunk), columns], preferred_element_type=jnp.float32
            )
            if h == 0:
                total[:, columns] = value
            else:
                total[:, columns] += value

    for h in range(2):
        for k in range(4 * h, 4 * h + 4):
            if k > 0:
                gather_wait(k)
                sibling_copy(k).start()
        for k in range(4 * h, 4 * h + 4):
            sibling_wait(k)
        draft(h)

    @pl.loop(1, n_req)
    def _(i):
        source = lax.rem(r + n_req - i, n_req)
        pltpu.make_async_remote_copy(
            src_ref=foll.at[source], dst_ref=foll.at[source],
            send_sem=fo_send.at[i], recv_sem=fo_recv.at[i],
            device_id={"req": source}, device_id_type=MESH,
        ).wait_recv()

    foll_copy.wait()
    for h in range(2):
        loss_grad(h)
    for h in range(2):
        project(h)
    out_copy = pltpu.make_async_copy(total, out_ref, io_sem.at[3])
    out_copy.start()

    sibling_copy(0).wait_send()
    for k in range(1, 8):
        gather_copy(k).wait_send()
        sibling_copy(k).wait_send()

    @pl.loop(1, n_req)
    def _(i):
        foll_exchange(i).wait_send()

    for h in range(2):

        @pl.loop(1, n_tp)
        def _(i):
            rs_copy(h, i).wait_send()
            gg_copy(h, i).wait_send()

    out_copy.wait()


def gradient(used, foll, w_flat, n_tp):
    block, features = used.shape
    outs = w_flat.shape[0]
    width = outs // n_tp
    chunk = 8 * block
    any_spec = pl.BlockSpec(memory_space=pl.ANY)
    dma = pltpu.SemaphoreType.DMA
    return pl.pallas_call(
        functools.partial(gradient_kernel, n_tp),
        out_shape=jax.ShapeDtypeStruct((outs, features), jnp.float32),
        in_specs=[any_spec] * 3,
        out_specs=any_spec,
        scratch_shapes=[
            pltpu.VMEM((2 * chunk, features), jnp.bfloat16),
            pltpu.VMEM((outs, features), jnp.bfloat16),
            pltpu.VMEM((16, width, 128), jnp.bfloat16),
            pltpu.VMEM((8 * 128, chunk), jnp.bfloat16),
            pltpu.VMEM((2, outs, chunk), jnp.bfloat16),
            pltpu.VMEM((2, n_tp, width, chunk), jnp.bfloat16),
            pltpu.VMEM((2, outs, chunk), jnp.bfloat16),
            pltpu.VMEM((outs, features), jnp.float32),
            dma((4,)), dma((8,)), dma((8,)), dma((8,)), dma((8,)), dma((16,)), dma((16,)),
            dma((2, n_tp)), dma((2, n_tp)), dma((2, n_tp)), dma((2, n_tp)),
        ],
        compiler_params=pltpu.CompilerParams(
            collective_id=0, has_side_effects=True, vmem_limit_bytes=40 * 2**20
        ),
        name="gradient",
    )(used, foll, w_flat)


def shards(query, k_cache, v_cache, ctx_len, residual, accepted, w_draft):
    requests, new_tokens, heads, head_dim = query.shape
    slots = k_cache.shape[2]
    hidden, used, foll = attention(
        query.reshape(requests, new_tokens * heads, head_dim),
        k_cache.reshape(requests, slots, head_dim),
        v_cache.reshape(requests, slots, head_dim),
        ctx_len, residual, accepted,
    )
    features, groups, width = w_draft.shape
    w_flat = w_draft.transpose(1, 2, 0).reshape(groups * width, features)
    grad = gradient(used, foll, w_flat, groups)
    return hidden, grad.reshape(groups, width, features).transpose(2, 0, 1)


def solution(mesh):
    placed = (
        P("req", None, "tp", None),
        P("req", "tp", None, None),
        P("req", "tp", None, None),
        P("req"),
        P("req", "tp"),
        P(),
        P("tp", None, "req"),
    )
    return jax.shard_map(
        shards,
        mesh=mesh,
        in_specs=placed,
        out_specs=(P("req", "tp"), P("tp", None, "req")),
        check_vma=False,
    )
```

```python
import jax
import jax.numpy as jnp
from jax import lax
from jax.experimental import pallas as pl
from jax.experimental.pallas import tpu as pltpu
from jax.sharding import PartitionSpec as P

QLEN = 6
LOG2_E = 1.4426950408889634
GROUP = 8
USED_PER_BLOCK = 80
SHORT = 256
BATCH = 16

MESH = pl.DeviceIdType.MESH


def attend(queries, keys, values, length, scale):
    slots = keys.shape[0]
    scores = lax.dot_general(
        queries, keys, (((1,), (1,)), ((), ())), preferred_element_type=jnp.float32
    ) * (scale * LOG2_E)
    rows, features = queries.shape
    position = lax.broadcasted_iota(jnp.int32, (rows, slots), 1)
    verified = lax.broadcasted_iota(jnp.int32, (rows, slots), 0) // GROUP
    scores = jnp.where(position < verified + (length - QLEN + 1), scores, -jnp.inf)
    top = jnp.max(scores, axis=-1, keepdims=True)
    weights = jnp.exp2(scores - top).astype(jnp.bfloat16)
    values = jnp.concatenate([values, jnp.ones((slots, features), jnp.bfloat16)], axis=1)
    mixed = jnp.dot(weights, values, preferred_element_type=jnp.float32)
    return mixed[:, :features] / mixed[:, features:]


def attention_kernel(
    ctx_ref, accepted_ref, q_hbm, k_hbm, v_hbm, res_hbm,
    hidden_hbm, used_ref, foll_ref,
    q_buf, k_buf, v_buf, res_buf, att_buf, hid_buf, k_sem, v_sem, k_more, v_more, io_sem,
):
    requests, slots, head_dim = k_hbm.shape
    rows = q_buf.shape[1]
    scale = head_dim ** (-0.5)
    batches = requests // BATCH
    q_copy = pltpu.make_async_copy(q_hbm, q_buf, io_sem.at[0])
    res_copy = pltpu.make_async_copy(res_hbm, res_buf, io_sem.at[1])
    q_copy.start()

    def short_copies(b):
        span = (pl.ds(b * BATCH, BATCH), pl.ds(0, SHORT))
        return (
            pltpu.make_async_copy(k_hbm.at[span], k_buf.at[span], k_sem.at[b]),
            pltpu.make_async_copy(v_hbm.at[span], v_buf.at[span], v_sem.at[b]),
        )

    def more_copies(r):
        span = (r, pl.ds(SHORT, slots - SHORT))
        return (
            pltpu.make_async_copy(k_hbm.at[span], k_buf.at[span], k_more.at[r]),
            pltpu.make_async_copy(v_hbm.at[span], v_buf.at[span], v_more.at[r]),
        )

    for b in range(batches):
        for copy in short_copies(b):
            copy.start()
    res_copy.start()

    @pl.loop(0, requests)
    def _(r):
        @pl.when(ctx_ref[r] > SHORT)
        def _():
            for copy in more_copies(r):
                copy.start()

    q_copy.wait()

    @pl.loop(0, batches)
    def _(b):
        for copy in short_copies(b):
            copy.wait()
        for j in range(BATCH):
            r = b * BATCH + j
            att_buf[pl.ds(pl.multiple_of(r * rows, rows), rows), :] = attend(
                q_buf[r], k_buf[r, 0:SHORT], v_buf[r, 0:SHORT], ctx_ref[r], scale
            )

    @pl.loop(0, requests)
    def _(r):
        @pl.when(ctx_ref[r] > SHORT)
        def _():
            for copy in more_copies(r):
                copy.wait()
            att_buf[pl.ds(pl.multiple_of(r * rows, rows), rows), :] = attend(
                q_buf[r], k_buf[r], v_buf[r], ctx_ref[r], scale
            )

    res_copy.wait()
    all_rows = requests * QLEN
    for h in range(GROUP):
        columns = pl.ds(h * head_dim, head_dim)
        mixed = att_buf[pl.ds(h, all_rows, stride=GROUP), :]
        hid_buf[:, columns] = (res_buf[:, columns].astype(jnp.float32) + mixed).astype(jnp.bfloat16)
    hidden_copy = pltpu.make_async_copy(hid_buf, hidden_hbm, io_sem.at[2])
    hidden_copy.start()

    row = lax.broadcasted_iota(jnp.int32, (1, all_rows), 1)
    request = row // QLEN
    verified = row - request * QLEN
    base = lax.axis_index("req") * requests
    place = jnp.full((1, all_rows), -1, jnp.int32)
    next_place = place
    before = jnp.int32(0)
    for r in range(requests):
        count = accepted_ref[base + r]
        mine = request == r
        place = jnp.where(mine & (verified < count), before + verified, place)
        next_place = jnp.where(
            mine & (verified >= 1) & (verified <= count), before + verified - 1, next_place
        )
        before = before + count
    hidden = hid_buf[...]
    want = lax.broadcasted_iota(jnp.int32, (used_ref.shape[0], all_rows), 0)
    pick = (want == place).astype(jnp.float32).astype(jnp.bfloat16)
    used_ref[...] = jnp.dot(pick, hidden, preferred_element_type=jnp.float32).astype(jnp.bfloat16)
    want = lax.broadcasted_iota(jnp.int32, (foll_ref.shape[1], all_rows), 0)
    pick = (want == next_place).astype(jnp.float32).astype(jnp.bfloat16)
    following = jnp.dot(pick, hidden, preferred_element_type=jnp.float32)
    foll_ref[...] = following.T.astype(jnp.bfloat16)
    hidden_copy.wait()


def attention(query, k_cache, v_cache, ctx_len, residual, accepted):
    requests, slots, head_dim = k_cache.shape
    rows = query.shape[1]
    all_rows, features = residual.shape
    any_spec = pl.BlockSpec(memory_space=pl.ANY)
    smem = pl.BlockSpec(memory_space=pltpu.SMEM)
    vmem = pl.BlockSpec(memory_space=pltpu.VMEM)
    batches = requests // BATCH
    return pl.pallas_call(
        attention_kernel,
        out_shape=(
            jax.ShapeDtypeStruct((all_rows, features), jnp.bfloat16),
            jax.ShapeDtypeStruct((USED_PER_BLOCK, features), jnp.bfloat16),
            jax.ShapeDtypeStruct((features, 128), jnp.bfloat16),
        ),
        in_specs=[smem, smem, any_spec, any_spec, any_spec, any_spec],
        out_specs=(any_spec, vmem, vmem),
        scratch_shapes=[
            pltpu.VMEM((requests, rows, head_dim), jnp.bfloat16),
            pltpu.VMEM((requests, slots, head_dim), jnp.bfloat16),
            pltpu.VMEM((requests, slots, head_dim), jnp.bfloat16),
            pltpu.VMEM((all_rows, features), jnp.bfloat16),
            pltpu.VMEM((requests * rows, head_dim), jnp.float32),
            pltpu.VMEM((all_rows, features), jnp.bfloat16),
            pltpu.SemaphoreType.DMA((batches,)),
            pltpu.SemaphoreType.DMA((batches,)),
            pltpu.SemaphoreType.DMA((requests,)),
            pltpu.SemaphoreType.DMA((requests,)),
            pltpu.SemaphoreType.DMA((3,)),
        ],
        compiler_params=pltpu.CompilerParams(vmem_limit_bytes=60 * 2**20),
        name="attention",
    )(ctx_len, accepted, query, k_cache, v_cache, residual)


SOURCES = ((0, 0), (0, 1), (0, 3), (0, 2), (1, 0), (1, 1), (1, 3), (1, 2))
PIECES = ((0, 48), (48, 32))
CHUNKS = (
    ((0, 1, 2, 3), ((0, 384, "x"), (384, 256, "y"))),
    ((4, 5, 6), ((640, 256, "x"), (896, 128, "y"))),
    ((7,), ((1024, 128, "x"), (1152, 128, "y"))),
)
PARTS = tuple(part for _, parts in CHUNKS for part in parts)


def gradient_kernel(
    used_ref, foll_ref, w_ref, out_ref,
    hid, w_buf, foll, place, following, part, first_x, first_y, half, own, second, grad, total,
    io_sem, g_send, g_recv, sib_send, sib_recv, fo_send, fo_recv,
    s1_send, s1_recv, s2_send, s2_recv, a1_send, a1_recv, a2_send, a2_recv,
):
    r = lax.axis_index("req")
    t = lax.axis_index("tp")
    core = lax.rem(r, 2)
    z = lax.rem(r // 2, 4)
    y_hi = r // 8
    x = lax.rem(t, 4)
    y_lo = t // 4
    other = 1 - y_lo
    block, features = used_ref.shape
    width = foll.shape[1]
    rows_all = hid.shape[0]

    def req_at(dy, dz, dc):
        return (lax.rem(y_hi + dy, 2) * 4 + lax.rem(z + 4 + dz, 4)) * 2 + lax.rem(core + dc, 2)

    def tp_x(i):
        return {"tp": y_lo * 4 + lax.rem(x + i, 4)}

    tp_y = {"tp": other * 4 + x}

    def remote(src, dst, send, recv, device):
        return pltpu.make_async_remote_copy(
            src_ref=src, dst_ref=dst, send_sem=send, recv_sem=recv,
            device_id=device, device_id_type=MESH,
        )

    w_copy = pltpu.make_async_copy(w_ref, w_buf, io_sem.at[0])
    own_copy = pltpu.make_async_copy(used_ref, hid.at[pl.ds(0, block)], io_sem.at[1])
    foll_copy = pltpu.make_async_copy(
        foll_ref.at[pl.ds(pl.multiple_of(r * width, width), width)], foll.at[0], io_sem.at[2]
    )
    own_copy.start()
    w_copy.start()
    foll_copy.start()

    barrier = pltpu.get_barrier_semaphore()
    for dy, dz in SOURCES:
        for dc in range(2):
            if (dy, dz, dc) != (0, 0, 0):
                pl.semaphore_signal(
                    barrier, inc=1, device_id={"req": req_at(dy, dz, dc)}, device_id_type=MESH
                )
    for i in range(1, 4):
        pl.semaphore_signal(barrier, inc=1, device_id=tp_x(i), device_id_type=MESH)
    pl.semaphore_signal(barrier, inc=1, device_id=tp_y, device_id_type=MESH)
    pl.semaphore_wait(barrier, 19)

    def shard(k, p):
        start, rows = PIECES[p]
        return hid.at[pl.ds(2 * block * k + start, rows)]

    def gather(k, p):
        start, rows = PIECES[p]
        mine = used_ref.at[pl.ds(start, rows)]
        if k == 1:
            src, target = mine, (0, -1)
        elif k == 2:
            src, target = mine, (0, 1)
        elif k == 3:
            src, target = (shard(2, 0), (0, 1)) if p == 0 else (shard(1, 1), (0, -1))
        elif k == 4:
            src, target = mine, (1, 0)
        elif k == 5:
            src, target = shard(4, p), (0, -1)
        elif k == 6:
            src, target = shard(4, p), (0, 1)
        else:
            src, target = (shard(6, 0), (0, 1)) if p == 0 else (shard(5, 1), (0, -1))
        return remote(
            src, shard(k, p), g_send.at[k, p], g_recv.at[k, p], {"req": req_at(*target, 0)}
        )

    def sibling(k):
        src = used_ref if k == 0 else hid.at[pl.ds(2 * block * k, block)]
        dst = hid.at[pl.ds(2 * block * k + block, block)]
        return remote(src, dst, sib_send.at[k], sib_recv.at[k], {"req": req_at(0, 0, 1)})

    for p in range(2):
        gather(2, p).start()
        gather(1, 1 - p).start()
        gather(4, p).start()
    sibling(0).start()

    half_rows = rows_all // 2

    @pl.loop(0, 8)
    def _(s):
        j = lax.broadcasted_iota(jnp.int32, (128, half_rows), 0)
        column = lax.broadcasted_iota(jnp.int32, (128, half_rows), 1)
        hit = (column == s * block + j) & (j < block)
        place[pl.ds(pl.multiple_of(s * 128, 128), 128), :] = hit.astype(jnp.float32).astype(
            jnp.bfloat16
        )

    own_copy.wait()
    w_copy.wait()

    def foll_exchange(k, dc):
        dy, dz = SOURCES[k]
        target = req_at(dy, -dz, dc)
        src = foll_ref.at[pl.ds(pl.multiple_of(target * width, width), width)]
        j = 2 * k + dc
        return remote(src, foll.at[j], fo_send.at[j], fo_recv.at[j], {"req": target})

    foll_peers = [(k, dc) for k in range(8) for dc in range(2) if (k, dc) != (0, 0)]

    def lanes(f):
        return pl.ds(PARTS[f][0], PARTS[f][1])

    def sum_first(f, i):
        if i:
            src = part.at[:, lax.rem(x + i, 4), :, lanes(f)]
            return remote(
                src, first_x.at[i - 1, :, :, lanes(f)], s1_send.at[f, i], s1_recv.at[f, i], tp_x(i)
            )
        src = part.at[other, :, :, lanes(f)]
        return remote(src, first_y.at[:, :, lanes(f)], s1_send.at[f, 0], s1_recv.at[f, 0], tp_y)

    def sum_second(f, i):
        slot = (i - 1) % 4
        src, dst = half.at[slot, :, lanes(f)], second.at[slot, :, lanes(f)]
        device = tp_x(i) if i else tp_y
        return remote(src, dst, s2_send.at[f, i], s2_recv.at[f, i], device)

    def grad_first(f, i):
        mine = grad.at[y_lo, x, :, lanes(f)]
        return remote(mine, mine, a1_send.at[f, i], a1_recv.at[f, i], tp_x(i) if i else tp_y)

    def grad_first_wait(f, i):
        theirs = grad.at[y_lo, lax.rem(x + 4 - i, 4), :, lanes(f)] if i else grad.at[
            other, x, :, lanes(f)
        ]
        remote(
            theirs, theirs, a1_send.at[f, i], a1_recv.at[f, i], tp_x(i) if i else tp_y
        ).wait_recv()

    def grad_second(f, i):
        if PARTS[f][2] == "x":
            mine, device = grad.at[other, x, :, lanes(f)], tp_x(i)
        else:
            mine, device = grad.at[y_lo, lax.rem(x + 4 - i, 4), :, lanes(f)], tp_y
        return remote(mine, mine, a2_send.at[f, i], a2_recv.at[f, i], device)

    def grad_second_wait(f, i):
        theirs = grad.at[other, lax.rem(x + 4 - i, 4), :, lanes(f)]
        remote(theirs, theirs, a2_send.at[f, i], a2_recv.at[f, i], tp_y).wait_recv()

    def draft(c):
        parts = CHUNKS[c][1]
        start, stop = parts[0][0], parts[-1][0] + parts[-1][1]
        while start < stop:
            step = min(256, stop - start)
            value = lax.dot_general(
                w_buf[...], hid[pl.ds(start, step), :], (((1,), (1,)), ((), ())),
                preferred_element_type=jnp.float32,
            )
            part[:, :, :, pl.ds(start, step)] = value.astype(jnp.bfloat16).reshape(
                part.shape[:3] + (step,)
            )
            start += step

    def peers(f, stage):
        return (1, 2, 3) if (PARTS[f][2] == "x") == (stage == 0) else (0,)

    def parts_of(c):
        return [f for f in range(len(PARTS)) if PARTS[f] in CHUNKS[c][1]]

    def start_first(c):
        draft(c)
        for f in parts_of(c):
            for i in peers(f, 0):
                sum_first(f, i).start()

    def start_second(c):
        for f in parts_of(c):
            n = lanes(f)
            for i in peers(f, 0):
                sum_first(f, i).wait_recv()
            if PARTS[f][2] == "x":

                def summed(g):
                    value = part[g, x, :, n].astype(jnp.float32)
                    for i in range(3):
                        value = value + first_x[i, g, :, n].astype(jnp.float32)
                    return value

                half[3, :, n] = summed(other).astype(jnp.bfloat16)
                sum_second(f, 0).start()
                own[:, n] = summed(y_lo)
            else:

                def summed(g):
                    return part[y_lo, g, :, n].astype(jnp.float32) + first_y[g, :, n].astype(
                        jnp.float32
                    )

                for i in range(1, 4):
                    half[i - 1, :, n] = summed(lax.rem(x + i, 4)).astype(jnp.bfloat16)
                    sum_second(f, i).start()
                own[:, n] = summed(x)

    def start_grad(c):
        for f in parts_of(c):
            n = lanes(f)
            value = own[:, n]
            for i in peers(f, 1):
                sum_second(f, i).wait_recv()
                value = value + second[(i - 1) % 4, :, n].astype(jnp.float32)
            value = (value - following[:, n]) / QLEN
            grad[y_lo, x, :, n] = value.astype(jnp.bfloat16)
            for i in range(4):
                grad_first(f, i).start()

    def forward_grad(c):
        for f in parts_of(c):
            if PARTS[f][2] == "x":
                grad_first_wait(f, 0)
                for i in range(1, 4):
                    grad_second(f, i).start()
            else:
                for i in range(1, 4):
                    grad_first_wait(f, i)
                    grad_second(f, i).start()

    def project(c, last):
        for f in parts_of(c):
            if PARTS[f][2] == "x":
                for i in range(1, 4):
                    grad_first_wait(f, i)
            else:
                grad_first_wait(f, 0)
            for i in range(1, 4):
                grad_second_wait(f, i)
        parts = CHUNKS[c][1]
        start = parts[0][0]
        rows = parts[-1][0] + parts[-1][1] - start
        tile = min(256, features)
        for n in range(features // tile):
            columns = pl.ds(n * tile, tile)
            value = jnp.dot(
                grad[:, :, :, pl.ds(start, rows)].reshape(total.shape[0], rows),
                hid[pl.ds(start, rows), columns],
                preferred_element_type=jnp.float32,
            )
            if c == 0:
                total[:, columns] = value
            else:
                total[:, columns] += value
            if last:
                out_copy(n).start()

    def out_copy(n):
        tile = min(256, features)
        span = (pl.ds(0, total.shape[0]), pl.ds(n * tile, tile))
        return pltpu.make_async_copy(total.at[span], out_ref.at[span], io_sem.at[3 + n])

    gather(2, 0).wait_recv()
    gather(3, 0).start()
    gather(1, 1).wait_recv()
    gather(3, 1).start()
    gather(2, 1).wait_recv()
    sibling(2).start()
    gather(1, 0).wait_recv()
    sibling(1).start()
    for p in range(2):
        gather(4, p).wait_recv()
        gather(6, p).start()
        gather(5, p).start()
    sibling(4).start()
    for p in range(2):
        gather(3, p).wait_recv()
    sibling(3).start()
    for k in CHUNKS[0][0]:
        sibling(k).wait_recv()
    start_first(0)
    gather(6, 0).wait_recv()
    gather(7, 0).start()
    gather(5, 1).wait_recv()
    gather(7, 1).start()
    gather(6, 1).wait_recv()
    sibling(6).start()
    gather(5, 0).wait_recv()
    sibling(5).start()
    for k, dc in foll_peers:
        foll_exchange(k, dc).start()
    for k in CHUNKS[1][0]:
        sibling(k).wait_recv()
    start_first(1)
    for p in range(2):
        gather(7, p).wait_recv()
    sibling(7).start()
    sibling(7).wait_recv()
    start_first(2)
    start_second(0)

    foll_copy.wait()
    for k, dc in foll_peers:
        foll_exchange(k, dc).wait_recv()
    for h in range(2):
        rows = jnp.concatenate([foll[8 * h + s] for s in range(8)], axis=1)
        following[:, pl.ds(h * half_rows, half_rows)] = jnp.dot(
            rows, place[...], preferred_element_type=jnp.float32
        )

    start_second(1)
    start_grad(0)
    start_second(2)
    forward_grad(0)
    start_grad(1)
    start_grad(2)
    forward_grad(1)
    forward_grad(2)
    project(0, False)
    project(1, False)
    project(2, True)

    for k in range(1, 8):
        for p in range(2):
            gather(k, p).wait_send()
    for k in range(8):
        sibling(k).wait_send()
    for k, dc in foll_peers:
        foll_exchange(k, dc).wait_send()
    for f in range(len(PARTS)):
        for i in peers(f, 0):
            sum_first(f, i).wait_send()
        for i in peers(f, 1):
            sum_second(f, i).wait_send()
        for i in range(4):
            grad_first(f, i).wait_send()
        for i in range(1, 4):
            grad_second(f, i).wait_send()
    for n in range(features // min(256, features)):
        out_copy(n).wait()


def gradient(used, foll, w_flat, n_tp):
    block, features = used.shape
    outs = w_flat.shape[0]
    width = outs // n_tp
    rows = 16 * block
    parts = len(PARTS)
    any_spec = pl.BlockSpec(memory_space=pl.ANY)
    dma = pltpu.SemaphoreType.DMA
    return pl.pallas_call(
        gradient_kernel,
        out_shape=jax.ShapeDtypeStruct((outs, features), jnp.float32),
        in_specs=[any_spec] * 3,
        out_specs=any_spec,
        scratch_shapes=[
            pltpu.VMEM((rows, features), jnp.bfloat16),
            pltpu.VMEM((outs, features), jnp.bfloat16),
            pltpu.VMEM((16, width, 128), jnp.bfloat16),
            pltpu.VMEM((8 * 128, rows // 2), jnp.bfloat16),
            pltpu.VMEM((width, rows), jnp.float32),
            pltpu.VMEM((2, 4, width, rows), jnp.bfloat16),
            pltpu.VMEM((3, 2, width, rows), jnp.bfloat16),
            pltpu.VMEM((4, width, rows), jnp.bfloat16),
            pltpu.VMEM((4, width, rows), jnp.bfloat16),
            pltpu.VMEM((width, rows), jnp.float32),
            pltpu.VMEM((4, width, rows), jnp.bfloat16),
            pltpu.VMEM((2, 4, width, rows), jnp.bfloat16),
            pltpu.VMEM((outs, features), jnp.float32),
            dma((7,)), dma((8, 2)), dma((8, 2)), dma((8,)), dma((8,)), dma((16,)), dma((16,)),
            dma((parts, 4)), dma((parts, 4)), dma((parts, 4)), dma((parts, 4)),
            dma((parts, 4)), dma((parts, 4)), dma((parts, 4)), dma((parts, 4)),
        ],
        compiler_params=pltpu.CompilerParams(
            collective_id=0, has_side_effects=True, vmem_limit_bytes=56 * 2**20
        ),
        name="gradient",
    )(used, foll, w_flat)


def shards(query, k_cache, v_cache, ctx_len, residual, accepted, w_draft):
    requests, new_tokens, heads, head_dim = query.shape
    slots = k_cache.shape[2]
    hidden, used, foll = attention(
        query.reshape(requests, new_tokens * heads, head_dim),
        k_cache.reshape(requests, slots, head_dim),
        v_cache.reshape(requests, slots, head_dim),
        ctx_len, residual, accepted,
    )
    features, groups, width = w_draft.shape
    w_flat = w_draft.transpose(1, 2, 0).reshape(groups * width, features)
    grad = gradient(used, foll, w_flat, groups)
    return hidden, grad.reshape(groups, width, features).transpose(2, 0, 1)


def solution(mesh):
    placed = (
        P("req", None, "tp", None),
        P("req", "tp", None, None),
        P("req", "tp", None, None),
        P("req"),
        P("req", "tp"),
        P(),
        P("tp", None, "req"),
    )
    return jax.shard_map(
        shards,
        mesh=mesh,
        in_specs=placed,
        out_specs=(P("req", "tp"), P("tp", None, "req")),
        check_vma=False,
    )
```

```python
import jax
import jax.numpy as jnp
from jax import lax
from jax.experimental import pallas as pl
from jax.experimental.pallas import tpu as pltpu
from jax.sharding import PartitionSpec as P

QLEN = 6
LOG2_E = 1.4426950408889634
GROUP = 8
USED_PER_BLOCK = 80
SHORT = 256
BATCH = 16

MESH = pl.DeviceIdType.MESH


def attend(queries, keys, values, length, scale):
    slots = keys.shape[0]
    scores = lax.dot_general(
        queries, keys, (((1,), (1,)), ((), ())), preferred_element_type=jnp.float32
    ) * (scale * LOG2_E)
    rows, features = queries.shape
    position = lax.broadcasted_iota(jnp.int32, (rows, slots), 1)
    verified = lax.broadcasted_iota(jnp.int32, (rows, slots), 0) // GROUP
    scores = jnp.where(position < verified + (length - QLEN + 1), scores, -jnp.inf)
    top = jnp.max(scores, axis=-1, keepdims=True)
    weights = jnp.exp2(scores - top).astype(jnp.bfloat16)
    values = jnp.concatenate([values, jnp.ones((slots, features), jnp.bfloat16)], axis=1)
    mixed = jnp.dot(weights, values, preferred_element_type=jnp.float32)
    return mixed[:, :features] / mixed[:, features:]


def attention_kernel(
    ctx_ref, accepted_ref, q_hbm, k_hbm, v_hbm, res_hbm,
    hidden_hbm, used_ref, foll_ref,
    q_buf, k_buf, v_buf, res_buf, att_buf, hid_buf, pick_buf, k_sem, v_sem, k_more, v_more, io_sem,
):
    requests, slots, head_dim = k_hbm.shape
    rows = q_buf.shape[1]
    scale = head_dim ** (-0.5)
    batches = requests // BATCH
    all_rows = requests * QLEN
    q_copy = pltpu.make_async_copy(q_hbm, q_buf, io_sem.at[0])
    res_copy = pltpu.make_async_copy(res_hbm, res_buf, io_sem.at[1])
    q_copy.start()

    def short_copies(b):
        span = (pl.ds(b * BATCH, BATCH), pl.ds(0, SHORT))
        return (
            pltpu.make_async_copy(k_hbm.at[span], k_buf.at[span], k_sem.at[b]),
            pltpu.make_async_copy(v_hbm.at[span], v_buf.at[span], v_sem.at[b]),
        )

    def more_copies(r):
        span = (r, pl.ds(SHORT, slots - SHORT))
        return (
            pltpu.make_async_copy(k_hbm.at[span], k_buf.at[span], k_more.at[r]),
            pltpu.make_async_copy(v_hbm.at[span], v_buf.at[span], v_more.at[r]),
        )

    for b in range(batches):
        for copy in short_copies(b):
            copy.start()
    res_copy.start()

    @pl.loop(0, requests)
    def _(r):
        @pl.when(ctx_ref[r] > SHORT)
        def _():
            for copy in more_copies(r):
                copy.start()

    row = lax.broadcasted_iota(jnp.int32, (1, all_rows), 1)
    request = row // QLEN
    verified = row - request * QLEN
    base = lax.axis_index("req") * requests
    place = jnp.full((1, all_rows), -1, jnp.int32)
    next_place = place
    before = jnp.int32(0)
    for r in range(requests):
        count = accepted_ref[base + r]
        mine = request == r
        place = jnp.where(mine & (verified < count), before + verified, place)
        next_place = jnp.where(
            mine & (verified >= 1) & (verified <= count), before + verified - 1, next_place
        )
        before = before + count
    want = lax.broadcasted_iota(jnp.int32, (used_ref.shape[0], all_rows), 0)
    pick_buf[0] = (want == place).astype(jnp.float32).astype(jnp.bfloat16)
    pick_buf[1] = (want == next_place).astype(jnp.float32).astype(jnp.bfloat16)

    q_copy.wait()

    @pl.loop(0, batches)
    def _(b):
        for copy in short_copies(b):
            copy.wait()
        for j in range(BATCH):
            r = b * BATCH + j
            att_buf[pl.ds(pl.multiple_of(r * rows, rows), rows), :] = attend(
                q_buf[r], k_buf[r, 0:SHORT], v_buf[r, 0:SHORT], ctx_ref[r], scale
            )

    @pl.loop(0, requests)
    def _(r):
        @pl.when(ctx_ref[r] > SHORT)
        def _():
            for copy in more_copies(r):
                copy.wait()
            att_buf[pl.ds(pl.multiple_of(r * rows, rows), rows), :] = attend(
                q_buf[r], k_buf[r], v_buf[r], ctx_ref[r], scale
            )

    res_copy.wait()
    for h in range(GROUP):
        columns = pl.ds(h * head_dim, head_dim)
        mixed = att_buf[pl.ds(h, all_rows, stride=GROUP), :]
        hid_buf[:, columns] = (res_buf[:, columns].astype(jnp.float32) + mixed).astype(jnp.bfloat16)
    hidden_copy = pltpu.make_async_copy(hid_buf, hidden_hbm, io_sem.at[2])
    hidden_copy.start()

    hidden = hid_buf[...]
    used_ref[...] = jnp.dot(pick_buf[0], hidden, preferred_element_type=jnp.float32).astype(jnp.bfloat16)
    foll_ref[...] = jnp.dot(pick_buf[1], hidden, preferred_element_type=jnp.float32).astype(jnp.bfloat16)
    hidden_copy.wait()


def attention(query, k_cache, v_cache, ctx_len, residual, accepted):
    requests, slots, head_dim = k_cache.shape
    rows = query.shape[1]
    all_rows, features = residual.shape
    hbm = pl.BlockSpec(memory_space=pl.ANY)
    smem = pl.BlockSpec(memory_space=pltpu.SMEM)
    vmem = pl.BlockSpec(memory_space=pltpu.VMEM)
    batches = requests // BATCH
    return pl.pallas_call(
        attention_kernel,
        out_shape=(
            jax.ShapeDtypeStruct((all_rows, features), jnp.bfloat16),
            jax.ShapeDtypeStruct((USED_PER_BLOCK, features), jnp.bfloat16),
            jax.ShapeDtypeStruct((USED_PER_BLOCK, features), jnp.bfloat16),
        ),
        in_specs=[smem, smem, hbm, hbm, hbm, hbm],
        out_specs=(hbm, vmem, vmem),
        scratch_shapes=[
            pltpu.VMEM((requests, rows, head_dim), jnp.bfloat16),
            pltpu.VMEM((requests, slots, head_dim), jnp.bfloat16),
            pltpu.VMEM((requests, slots, head_dim), jnp.bfloat16),
            pltpu.VMEM((all_rows, features), jnp.bfloat16),
            pltpu.VMEM((requests * rows, head_dim), jnp.float32),
            pltpu.VMEM((all_rows, features), jnp.bfloat16),
            pltpu.VMEM((2, USED_PER_BLOCK, all_rows), jnp.bfloat16),
            pltpu.SemaphoreType.DMA((batches,)),
            pltpu.SemaphoreType.DMA((batches,)),
            pltpu.SemaphoreType.DMA((requests,)),
            pltpu.SemaphoreType.DMA((requests,)),
            pltpu.SemaphoreType.DMA((3,)),
        ],
        compiler_params=pltpu.CompilerParams(vmem_limit_bytes=58 * 2**20),
        name="attention",
    )(ctx_len, accepted, query, k_cache, v_cache, residual)


SOURCES = ((0, 0), (0, 1), (0, 3), (1, 0), (0, 2), (1, 1), (1, 3), (1, 2))
CHUNKS = (
    ((0,), ((0, 128, "x"),)),
    ((1, 2, 3), ((128, 256, "x"), (384, 256, "y"))),
    ((4, 5, 6), ((640, 256, "x"), (896, 128, "y"))),
    ((7,), ((1024, 128, "x"), (1152, 128, "y"))),
)
PIECES = ((0, 48), (48, 32))
PARTS = tuple(part for _, parts in CHUNKS for part in parts)
DIRECT = (2, 6, 4, 5, 7, 1, 3)


def gradient_kernel(
    used_ref, foll_ref, w_ref, out_ref,
    hid, w_buf, foll, following, part, first_x, first_y, half, own, second, direct, grad, total,
    io_sem, g_send, g_recv, sib_send, sib_recv, fo_send, fo_recv,
    s1_send, s1_recv, s2_send, s2_recv, a1_send, a1_recv, a2_send, a2_recv,
    d1_send, d1_recv, d2_send, d2_recv,
):
    r = lax.axis_index("req")
    t = lax.axis_index("tp")
    core = lax.rem(r, 2)
    z = lax.rem(r // 2, 4)
    y_hi = r // 8
    x = lax.rem(t, 4)
    y_lo = t // 4
    other = 1 - y_lo
    block, features = used_ref.shape
    width = part.shape[2]
    rows_all = hid.shape[0]

    def req_at(dy, dz, dc):
        return (lax.rem(y_hi + dy, 2) * 4 + lax.rem(z + 4 + dz, 4)) * 2 + lax.rem(core + dc, 2)

    def tp_x(i):
        return {"tp": y_lo * 4 + lax.rem(x + i, 4)}

    tp_y = {"tp": other * 4 + x}

    def tp_diagonal(i):
        return {"tp": other * 4 + lax.rem(x + i, 4)}

    def remote(src, dst, send, recv, device):
        return pltpu.make_async_remote_copy(
            src_ref=src, dst_ref=dst, send_sem=send, recv_sem=recv,
            device_id=device, device_id_type=MESH,
        )

    w_copy = pltpu.make_async_copy(w_ref, w_buf, io_sem.at[0])
    own_copy = pltpu.make_async_copy(used_ref, hid.at[pl.ds(0, block)], io_sem.at[1])
    foll_copy = pltpu.make_async_copy(
        foll_ref.at[:, pl.ds(pl.multiple_of(r // 2 * 128, 128), 128)],
        foll.at[pl.ds(0, block)],
        io_sem.at[2],
    )
    own_copy.start()
    w_copy.start()
    foll_copy.start()

    barrier = pltpu.get_barrier_semaphore()
    for dy, dz in SOURCES:
        dc = int((dy, dz) == (0, 0))
        pl.semaphore_signal(
            barrier, inc=1, device_id={"req": req_at(dy, dz, dc)}, device_id_type=MESH
        )
    for i in range(1, 4):
        pl.semaphore_signal(barrier, inc=1, device_id=tp_x(i), device_id_type=MESH)
        pl.semaphore_signal(barrier, inc=1, device_id=tp_diagonal(i), device_id_type=MESH)
    pl.semaphore_signal(barrier, inc=1, device_id=tp_y, device_id_type=MESH)
    pl.semaphore_wait(barrier, 15)

    up, down, across = (0, 1), (0, -1), (1, 0)
    routes = {
        1: ((0, down), (0, down)), 2: ((0, up), (0, up)), 3: ((0, across), (0, across)),
        4: ((2, up), (1, down)), 5: ((3, down), (3, down)), 6: ((3, up), (3, up)),
        7: ((6, up), (5, down)),
    }

    def shard(k, p):
        start, rows = PIECES[p]
        return hid.at[pl.ds(2 * block * k + start, rows)]

    def gather(k, p):
        source, target = routes[k][p]
        start, rows = PIECES[p]
        return remote(
            shard(source, p) if source else used_ref.at[pl.ds(start, rows)], shard(k, p),
            g_send.at[k, p], g_recv.at[k, p], {"req": req_at(*target, 0)},
        )

    def sibling(k):
        src = used_ref if k == 0 else hid.at[pl.ds(2 * block * k, block)]
        dst = hid.at[pl.ds(2 * block * k + block, block)]
        return remote(src, dst, sib_send.at[k], sib_recv.at[k], {"req": req_at(0, 0, 1)})

    for p in range(2):
        gather(2, p).start()
        gather(1, 1 - p).start()
        gather(3, p).start()
    sibling(0).start()

    own_copy.wait()
    w_copy.wait()

    def foll_rows(j):
        return foll.at[pl.ds(j * block, block)]

    def foll_exchange(k):
        dy, dz = SOURCES[k]
        chip = lax.rem(y_hi + dy, 2) * 4 + lax.rem(z + 4 - dz, 4)
        src = foll_ref.at[:, pl.ds(pl.multiple_of(chip * 128, 128), 128)]
        return remote(
            src, foll_rows(2 * k), fo_send.at[2 * k], fo_recv.at[2 * k],
            {"req": req_at(dy, -dz, 0)},
        )

    def foll_sibling(k):
        j = 2 * k + 1
        return remote(
            foll_rows(2 * k), foll_rows(j), fo_send.at[j], fo_recv.at[j], {"req": req_at(0, 0, 1)}
        )

    def lanes(f):
        return pl.ds(PARTS[f][0], PARTS[f][1])

    def sum_first(f, i):
        if i:
            src = part.at[:, lax.rem(x + i, 4), :, lanes(f)]
            return remote(
                src, first_x.at[i - 1, :, :, lanes(f)], s1_send.at[f, i], s1_recv.at[f, i], tp_x(i)
            )
        src = part.at[other, :, :, lanes(f)]
        return remote(src, first_y.at[:, :, lanes(f)], s1_send.at[f, 0], s1_recv.at[f, 0], tp_y)

    def sum_direct(f, i):
        row, column = (y_lo, other)[i // 4], lax.rem(x + i, 4)
        src, dst = part.at[row, column, :, lanes(f)], direct.at[i - 1, :, lanes(f)]
        return remote(src, dst, d1_send.at[f, i], d1_recv.at[f, i], tp_at(i))

    def grad_direct(f, i):
        mine = grad.at[y_lo, x, :, lanes(f)]
        return remote(mine, mine, d2_send.at[f, i], d2_recv.at[f, i], tp_at(i))

    def grad_direct_wait(f, i):
        theirs = grad.at[(y_lo, other)[i // 4], lax.rem(x + 8 - i, 4), :, lanes(f)]
        remote(theirs, theirs, d2_send.at[f, i], d2_recv.at[f, i], tp_at(i)).wait_recv()

    def tp_at(i):
        return {"tp": (y_lo, other)[i // 4] * 4 + lax.rem(x + i, 4)}

    def is_direct(f):
        return PARTS[f][2] == "d"

    def sum_second(f, i):
        slot = (i - 1) % 4
        src, dst = half.at[slot, :, lanes(f)], second.at[slot, :, lanes(f)]
        device = tp_x(i) if i else tp_y
        return remote(src, dst, s2_send.at[f, i], s2_recv.at[f, i], device)

    def grad_first(f, i):
        mine = grad.at[y_lo, x, :, lanes(f)]
        return remote(mine, mine, a1_send.at[f, i], a1_recv.at[f, i], tp_x(i) if i else tp_y)

    def grad_first_wait(f, i):
        theirs = grad.at[y_lo, lax.rem(x + 4 - i, 4), :, lanes(f)] if i else grad.at[
            other, x, :, lanes(f)
        ]
        remote(
            theirs, theirs, a1_send.at[f, i], a1_recv.at[f, i], tp_x(i) if i else tp_y
        ).wait_recv()

    def grad_second(f, i):
        if PARTS[f][2] == "x":
            mine, device = grad.at[other, x, :, lanes(f)], tp_x(i)
        else:
            mine, device = grad.at[y_lo, lax.rem(x + 4 - i, 4), :, lanes(f)], tp_y
        return remote(mine, mine, a2_send.at[f, i], a2_recv.at[f, i], device)

    def grad_second_wait(f, i):
        theirs = grad.at[other, lax.rem(x + 4 - i, 4), :, lanes(f)]
        remote(theirs, theirs, a2_send.at[f, i], a2_recv.at[f, i], tp_y).wait_recv()

    def draft(c):
        parts = CHUNKS[c][1]
        start, stop = parts[0][0], parts[-1][0] + parts[-1][1]
        while start < stop:
            step = min(256, stop - start)
            value = lax.dot_general(
                w_buf[...], hid[pl.ds(start, step), :], (((1,), (1,)), ((), ())),
                preferred_element_type=jnp.float32,
            )
            part[:, :, :, pl.ds(start, step)] = value.astype(jnp.bfloat16).reshape(
                part.shape[:3] + (step,)
            )
            start += step

    def peers(f, stage):
        if is_direct(f):
            return ()
        return (1, 2, 3) if (PARTS[f][2] == "x") == (stage == 0) else (0,)

    def parts_of(c):
        return [f for f in range(len(PARTS)) if PARTS[f] in CHUNKS[c][1]]

    def start_first(c):
        draft(c)
        for f in parts_of(c):
            for i in peers(f, 0):
                sum_first(f, i).start()
            if is_direct(f):
                for i in DIRECT:
                    sum_direct(f, i).start()

    def start_second(c):
        for f in parts_of(c):
            n = lanes(f)
            if is_direct(f):
                continue
            for i in peers(f, 0):
                sum_first(f, i).wait_recv()
            if PARTS[f][2] == "x":

                def summed(g):
                    value = part[g, x, :, n].astype(jnp.float32)
                    for i in range(3):
                        value = value + first_x[i, g, :, n].astype(jnp.float32)
                    return value

                half[3, :, n] = summed(other).astype(jnp.bfloat16)
                sum_second(f, 0).start()
                own[:, n] = summed(y_lo)
            else:

                def summed(g):
                    return part[y_lo, g, :, n].astype(jnp.float32) + first_y[g, :, n].astype(
                        jnp.float32
                    )

                for i in range(1, 4):
                    half[i - 1, :, n] = summed(lax.rem(x + i, 4)).astype(jnp.bfloat16)
                    sum_second(f, i).start()
                own[:, n] = summed(x)

    def start_grad(c):
        for f in parts_of(c):
            n = lanes(f)
            if is_direct(f):
                value = part[y_lo, x, :, n].astype(jnp.float32)
                for i in DIRECT:
                    sum_direct(f, i).wait_recv()
                    value = value + direct[i - 1, :, n].astype(jnp.float32)
            else:
                value = own[:, n]
            for i in peers(f, 1):
                sum_second(f, i).wait_recv()
                value = value + second[(i - 1) % 4, :, n].astype(jnp.float32)
            value = (value - following[:, n]) / QLEN
            grad[y_lo, x, :, n] = value.astype(jnp.bfloat16)
            if is_direct(f):
                for i in DIRECT:
                    grad_direct(f, i).start()
                continue
            for i in range(4):
                grad_first(f, i).start()

    def forward_grad(c):
        for f in parts_of(c):
            if is_direct(f):
                continue
            if PARTS[f][2] == "x":
                grad_first_wait(f, 0)
                for i in range(1, 4):
                    grad_second(f, i).start()
            else:
                for i in range(1, 4):
                    grad_first_wait(f, i)
                    grad_second(f, i).start()

    def project(c):
        for f in parts_of(c):
            if is_direct(f):
                for i in DIRECT:
                    grad_direct_wait(f, i)
                continue
            if PARTS[f][2] == "x":
                for i in range(1, 4):
                    grad_first_wait(f, i)
            else:
                grad_first_wait(f, 0)
            for i in range(1, 4):
                grad_second_wait(f, i)
        start, rows = span_of(c)
        tile = min(256, features)
        for n in range(features // tile):
            columns = pl.ds(n * tile, tile)
            value = jnp.dot(
                grad[:, :, :, pl.ds(start, rows)].reshape(total.shape[0], rows),
                hid[pl.ds(start, rows), columns],
                preferred_element_type=jnp.float32,
            )
            if c == 0:
                total[:, columns] = value
            else:
                total[:, columns] += value
            if c == len(CHUNKS) - 1:
                out_copy(n).start()

    def span_of(c):
        parts = CHUNKS[c][1]
        return parts[0][0], parts[-1][0] + parts[-1][1] - parts[0][0]

    def out_copy(n):
        tile = min(256, features)
        span = (pl.ds(0, total.shape[0]), pl.ds(n * tile, tile))
        return pltpu.make_async_copy(total.at[span], out_ref.at[span], io_sem.at[3 + n])

    def arrive(c):
        for k in CHUNKS[c][0]:
            sibling(k).wait_recv()

    def following_of(half):
        span = rows_all // 2
        rows = foll[pl.ds(half * span, span), :].astype(jnp.float32).T
        return jnp.where(core == 0, rows[:width], rows[width:])

    arrive(0)
    start_first(0)
    gather(2, 0).wait_recv()
    gather(4, 0).start()
    gather(1, 1).wait_recv()
    gather(4, 1).start()
    gather(2, 1).wait_recv()
    sibling(2).start()
    gather(1, 0).wait_recv()
    sibling(1).start()
    for p in range(2):
        gather(3, p).wait_recv()
        gather(6, p).start()
        gather(5, p).start()
    sibling(3).start()
    start_second(0)
    arrive(1)
    start_first(1)
    for k in range(1, 8):
        foll_exchange(k).start()
    for p in range(2):
        gather(4, p).wait_recv()
    sibling(4).start()
    gather(6, 0).wait_recv()
    gather(7, 0).start()
    gather(5, 1).wait_recv()
    gather(7, 1).start()
    gather(6, 1).wait_recv()
    sibling(6).start()
    gather(5, 0).wait_recv()
    sibling(5).start()
    arrive(2)
    start_first(2)
    start_second(1)
    foll_copy.wait()
    foll_sibling(0).start()
    for k in range(1, 8):
        foll_exchange(k).wait_recv()
        foll_sibling(k).start()
    for p in range(2):
        gather(7, p).wait_recv()
    sibling(7).start()
    for k in range(8):
        foll_sibling(k).wait_recv()
    for h in range(2):
        following[:, pl.ds(h * (rows_all // 2), rows_all // 2)] = following_of(h)
    start_grad(0)
    arrive(3)
    start_first(3)
    start_grad(1)
    start_second(2)
    forward_grad(0)
    start_second(3)
    forward_grad(1)
    start_grad(2)
    start_grad(3)
    forward_grad(2)
    forward_grad(3)
    for c in range(len(CHUNKS)):
        project(c)

    for k in range(1, 8):
        for p in range(2):
            gather(k, p).wait_send()
    for k in range(8):
        sibling(k).wait_send()
    for k in range(8):
        if k:
            foll_exchange(k).wait_send()
        foll_sibling(k).wait_send()
    for f in range(len(PARTS)):
        if is_direct(f):
            for i in DIRECT:
                sum_direct(f, i).wait_send()
                grad_direct(f, i).wait_send()
            continue
        for i in peers(f, 0):
            sum_first(f, i).wait_send()
        for i in peers(f, 1):
            sum_second(f, i).wait_send()
        for i in range(4):
            grad_first(f, i).wait_send()
        for i in range(1, 4):
            grad_second(f, i).wait_send()
    for n in range(features // min(256, features)):
        out_copy(n).wait()


def gradient(used, foll, w_flat, n_tp):
    block, features = used.shape
    outs = w_flat.shape[0]
    width = outs // n_tp
    rows = 16 * block
    parts = len(PARTS)
    any_spec = pl.BlockSpec(memory_space=pl.ANY)
    dma = pltpu.SemaphoreType.DMA
    return pl.pallas_call(
        gradient_kernel,
        out_shape=jax.ShapeDtypeStruct((outs, features), jnp.float32),
        in_specs=[any_spec] * 3,
        out_specs=any_spec,
        scratch_shapes=[
            pltpu.VMEM((rows, features), jnp.bfloat16),
            pltpu.VMEM((outs, features), jnp.bfloat16),
            pltpu.VMEM((rows, 128), jnp.bfloat16),
            pltpu.VMEM((width, rows), jnp.float32),
            pltpu.VMEM((2, 4, width, rows), jnp.bfloat16),
            pltpu.VMEM((3, 2, width, rows), jnp.bfloat16),
            pltpu.VMEM((4, width, rows), jnp.bfloat16),
            pltpu.VMEM((4, width, rows), jnp.bfloat16),
            pltpu.VMEM((width, rows), jnp.float32),
            pltpu.VMEM((4, width, rows), jnp.bfloat16),
            pltpu.VMEM((7, width, rows), jnp.bfloat16),
            pltpu.VMEM((2, 4, width, rows), jnp.bfloat16),
            pltpu.VMEM((outs, features), jnp.float32),
            dma((7,)), dma((8, 2)), dma((8, 2)), dma((8,)), dma((8,)), dma((16,)), dma((16,)),
            dma((parts, 4)), dma((parts, 4)), dma((parts, 4)), dma((parts, 4)),
            dma((parts, 4)), dma((parts, 4)), dma((parts, 4)), dma((parts, 4)),
            dma((parts, 8)), dma((parts, 8)), dma((parts, 8)), dma((parts, 8)),
        ],
        compiler_params=pltpu.CompilerParams(
            collective_id=0, has_side_effects=True, vmem_limit_bytes=58 * 2**20
        ),
        name="gradient",
    )(used, foll, w_flat)


def shards(query, k_cache, v_cache, ctx_len, residual, accepted, w_draft):
    requests, new_tokens, heads, head_dim = query.shape
    slots = k_cache.shape[2]
    hidden, used, foll = attention(
        query.reshape(requests, new_tokens * heads, head_dim),
        k_cache.reshape(requests, slots, head_dim),
        v_cache.reshape(requests, slots, head_dim),
        ctx_len, residual, accepted,
    )
    features, groups, width = w_draft.shape
    w_flat = w_draft.transpose(1, 2, 0).reshape(groups * width, features)
    grad = gradient(used, foll, w_flat, groups)
    return hidden, grad.reshape(groups, width, features).transpose(2, 0, 1)


def solution(mesh):
    placed = (
        P("req", None, "tp", None),
        P("req", "tp", None, None),
        P("req", "tp", None, None),
        P("req"),
        P("req", "tp"),
        P(),
        P("tp", None, "req"),
    )
    return jax.shard_map(
        shards,
        mesh=mesh,
        in_specs=placed,
        out_specs=(P("req", "tp"), P("tp", None, "req")),
        check_vma=False,
    )
```

```python
import jax
import jax.numpy as jnp
from jax import lax
from jax.experimental import pallas as pl
from jax.experimental.pallas import tpu as pltpu
from jax.sharding import PartitionSpec as P

QLEN = 6
LOG2_E = 1.4426950408889634
GROUP = 8
USED_PER_BLOCK = 80
SHORT = 256
BATCH = 16

MESH = pl.DeviceIdType.MESH


def attend(queries, keys, values, length, scale):
    slots = keys.shape[0]
    scores = lax.dot_general(
        queries, keys, (((1,), (1,)), ((), ())), preferred_element_type=jnp.float32
    ) * (scale * LOG2_E)
    rows, features = queries.shape
    position = lax.broadcasted_iota(jnp.int32, (rows, slots), 1)
    verified = lax.broadcasted_iota(jnp.int32, (rows, slots), 0) // GROUP
    scores = jnp.where(position < verified + (length - QLEN + 1), scores, -jnp.inf)
    top = jnp.max(scores, axis=-1, keepdims=True)
    weights = jnp.exp2(scores - top).astype(jnp.bfloat16)
    values = jnp.concatenate([values, jnp.ones((slots, features), jnp.bfloat16)], axis=1)
    mixed = jnp.dot(weights, values, preferred_element_type=jnp.float32)
    return mixed[:, :features] / mixed[:, features:]


def attention_kernel(
    ctx_ref, accepted_ref, q_hbm, k_hbm, v_hbm, res_hbm,
    hidden_hbm, used_ref, foll_ref,
    q_buf, k_buf, v_buf, res_buf, att_buf, hid_buf, pick_buf, k_sem, v_sem, k_more, v_more, io_sem,
):
    requests, slots, head_dim = k_hbm.shape
    rows = q_buf.shape[1]
    scale = head_dim ** (-0.5)
    batches = requests // BATCH
    all_rows = requests * QLEN
    q_copy = pltpu.make_async_copy(q_hbm, q_buf, io_sem.at[0])
    res_copy = pltpu.make_async_copy(res_hbm, res_buf, io_sem.at[1])
    q_copy.start()

    def short_copies(b):
        span = (pl.ds(b * BATCH, BATCH), pl.ds(0, SHORT))
        return (
            pltpu.make_async_copy(k_hbm.at[span], k_buf.at[span], k_sem.at[b]),
            pltpu.make_async_copy(v_hbm.at[span], v_buf.at[span], v_sem.at[b]),
        )

    def more_copies(r):
        span = (r, pl.ds(SHORT, slots - SHORT))
        return (
            pltpu.make_async_copy(k_hbm.at[span], k_buf.at[span], k_more.at[r]),
            pltpu.make_async_copy(v_hbm.at[span], v_buf.at[span], v_more.at[r]),
        )

    for b in range(batches):
        for copy in short_copies(b):
            copy.start()
    res_copy.start()

    @pl.loop(0, requests)
    def _(r):
        @pl.when(ctx_ref[r] > SHORT)
        def _():
            for copy in more_copies(r):
                copy.start()

    row = lax.broadcasted_iota(jnp.int32, (1, all_rows), 1)
    request = row // QLEN
    verified = row - request * QLEN
    base = lax.axis_index("req") * requests
    place = jnp.full((1, all_rows), -1, jnp.int32)
    next_place = place
    before = jnp.int32(0)
    for r in range(requests):
        count = accepted_ref[base + r]
        mine = request == r
        place = jnp.where(mine & (verified < count), before + verified, place)
        next_place = jnp.where(
            mine & (verified >= 1) & (verified <= count), before + verified - 1, next_place
        )
        before = before + count
    want = lax.broadcasted_iota(jnp.int32, (used_ref.shape[0], all_rows), 0)
    pick_buf[0] = (want == place).astype(jnp.float32).astype(jnp.bfloat16)
    pick_buf[1] = (want == next_place).astype(jnp.float32).astype(jnp.bfloat16)

    q_copy.wait()

    @pl.loop(0, batches)
    def _(b):
        for copy in short_copies(b):
            copy.wait()
        for j in range(BATCH):
            r = b * BATCH + j
            att_buf[pl.ds(pl.multiple_of(r * rows, rows), rows), :] = attend(
                q_buf[r], k_buf[r, 0:SHORT], v_buf[r, 0:SHORT], ctx_ref[r], scale
            )

    @pl.loop(0, requests)
    def _(r):
        @pl.when(ctx_ref[r] > SHORT)
        def _():
            for copy in more_copies(r):
                copy.wait()
            att_buf[pl.ds(pl.multiple_of(r * rows, rows), rows), :] = attend(
                q_buf[r], k_buf[r], v_buf[r], ctx_ref[r], scale
            )

    res_copy.wait()
    for h in range(GROUP):
        columns = pl.ds(h * head_dim, head_dim)
        mixed = att_buf[pl.ds(h, all_rows, stride=GROUP), :]
        hid_buf[:, columns] = (res_buf[:, columns].astype(jnp.float32) + mixed).astype(jnp.bfloat16)
    hidden_copy = pltpu.make_async_copy(hid_buf, hidden_hbm, io_sem.at[2])
    hidden_copy.start()

    hidden = hid_buf[...]
    used_ref[...] = jnp.dot(pick_buf[0], hidden, preferred_element_type=jnp.float32).astype(jnp.bfloat16)
    foll_ref[...] = jnp.dot(pick_buf[1], hidden, preferred_element_type=jnp.float32).astype(jnp.bfloat16)
    hidden_copy.wait()


def attention(query, k_cache, v_cache, ctx_len, residual, accepted):
    requests, slots, head_dim = k_cache.shape
    rows = query.shape[1]
    all_rows, features = residual.shape
    hbm = pl.BlockSpec(memory_space=pl.ANY)
    smem = pl.BlockSpec(memory_space=pltpu.SMEM)
    vmem = pl.BlockSpec(memory_space=pltpu.VMEM)
    batches = requests // BATCH
    return pl.pallas_call(
        attention_kernel,
        out_shape=(
            jax.ShapeDtypeStruct((all_rows, features), jnp.bfloat16),
            jax.ShapeDtypeStruct((USED_PER_BLOCK, features), jnp.bfloat16),
            jax.ShapeDtypeStruct((USED_PER_BLOCK, features), jnp.bfloat16),
        ),
        in_specs=[smem, smem, hbm, hbm, hbm, hbm],
        out_specs=(hbm, vmem, vmem),
        scratch_shapes=[
            pltpu.VMEM((requests, rows, head_dim), jnp.bfloat16),
            pltpu.VMEM((requests, slots, head_dim), jnp.bfloat16),
            pltpu.VMEM((requests, slots, head_dim), jnp.bfloat16),
            pltpu.VMEM((all_rows, features), jnp.bfloat16),
            pltpu.VMEM((requests * rows, head_dim), jnp.float32),
            pltpu.VMEM((all_rows, features), jnp.bfloat16),
            pltpu.VMEM((2, USED_PER_BLOCK, all_rows), jnp.bfloat16),
            pltpu.SemaphoreType.DMA((batches,)),
            pltpu.SemaphoreType.DMA((batches,)),
            pltpu.SemaphoreType.DMA((requests,)),
            pltpu.SemaphoreType.DMA((requests,)),
            pltpu.SemaphoreType.DMA((3,)),
        ],
        compiler_params=pltpu.CompilerParams(vmem_limit_bytes=58 * 2**20),
        name="attention",
    )(ctx_len, accepted, query, k_cache, v_cache, residual)


SOURCES = ((0, 0), (0, 1), (0, 3), (1, 0), (0, 2), (1, 1), (1, 3), (1, 2))
CHUNKS = (
    ((0,), ((0, 128, "x"),)),
    ((1, 2, 3), ((128, 256, "x"), (384, 256, "y"))),
    ((4, 5, 6), ((640, 256, "x"), (896, 128, "y"))),
    ((7,), ((1024, 128, "x"), (1152, 128, "y"))),
)
PIECES = ((0, 48), (48, 32))
PARTS = tuple(part for _, parts in CHUNKS for part in parts)
DIRECT = (2, 6, 4, 5, 7, 1, 3)


def gradient_kernel(
    used_ref, foll_ref, w_ref, out_ref,
    hid, w_buf, foll, following, part, first_x, first_y, half, own, second, direct, grad, total,
    io_sem, g_send, g_recv, sib_send, sib_recv, fo_send, fo_recv,
    s1_send, s1_recv, s2_send, s2_recv, a1_send, a1_recv, a2_send, a2_recv,
    d1_send, d1_recv, d2_send, d2_recv,
):
    r = lax.axis_index("req")
    t = lax.axis_index("tp")
    core = lax.rem(r, 2)
    z = lax.rem(r // 2, 4)
    y_hi = r // 8
    x = lax.rem(t, 4)
    y_lo = t // 4
    other = 1 - y_lo
    block, features = used_ref.shape
    width = part.shape[2]
    rows_all = hid.shape[0]

    def req_at(dy, dz, dc):
        return (lax.rem(y_hi + dy, 2) * 4 + lax.rem(z + 4 + dz, 4)) * 2 + lax.rem(core + dc, 2)

    def tp_x(i):
        return {"tp": y_lo * 4 + lax.rem(x + i, 4)}

    tp_y = {"tp": other * 4 + x}

    def tp_diagonal(i):
        return {"tp": other * 4 + lax.rem(x + i, 4)}

    def remote(src, dst, send, recv, device):
        return pltpu.make_async_remote_copy(
            src_ref=src, dst_ref=dst, send_sem=send, recv_sem=recv,
            device_id=device, device_id_type=MESH,
        )

    w_copy = pltpu.make_async_copy(w_ref, w_buf, io_sem.at[0])
    own_copy = pltpu.make_async_copy(used_ref, hid.at[pl.ds(0, block)], io_sem.at[1])
    foll_copy = pltpu.make_async_copy(
        foll_ref.at[:, pl.ds(pl.multiple_of(r // 2 * 128, 128), 128)],
        foll.at[pl.ds(0, block)],
        io_sem.at[2],
    )
    own_copy.start()
    w_copy.start()
    foll_copy.start()

    barrier = pltpu.get_barrier_semaphore()
    for dy, dz in SOURCES:
        dc = int((dy, dz) == (0, 0))
        pl.semaphore_signal(
            barrier, inc=1, device_id={"req": req_at(dy, dz, dc)}, device_id_type=MESH
        )
    for i in range(1, 4):
        pl.semaphore_signal(barrier, inc=1, device_id=tp_x(i), device_id_type=MESH)
        pl.semaphore_signal(barrier, inc=1, device_id=tp_diagonal(i), device_id_type=MESH)
    pl.semaphore_signal(barrier, inc=1, device_id=tp_y, device_id_type=MESH)
    pl.semaphore_wait(barrier, 15)

    up, down, across = (0, 1), (0, -1), (1, 0)
    routes = {
        1: ((0, down), (0, down)), 2: ((0, up), (0, up)), 3: ((0, across), (0, across)),
        4: ((2, up), (1, down)), 5: ((3, down), (3, down)), 6: ((3, up), (3, up)),
        7: ((6, up), (5, down)),
    }

    def shard(k, p):
        start, rows = PIECES[p]
        return hid.at[pl.ds(2 * block * k + start, rows)]

    def gather(k, p):
        source, target = routes[k][p]
        start, rows = PIECES[p]
        return remote(
            shard(source, p) if source else used_ref.at[pl.ds(start, rows)], shard(k, p),
            g_send.at[k, p], g_recv.at[k, p], {"req": req_at(*target, 0)},
        )

    def sibling(k):
        src = used_ref if k == 0 else hid.at[pl.ds(2 * block * k, block)]
        dst = hid.at[pl.ds(2 * block * k + block, block)]
        return remote(src, dst, sib_send.at[k], sib_recv.at[k], {"req": req_at(0, 0, 1)})

    for p in range(2):
        gather(2, p).start()
        gather(1, 1 - p).start()
        gather(3, p).start()
    sibling(0).start()

    own_copy.wait()
    w_copy.wait()

    def foll_rows(j):
        return foll.at[pl.ds(j * block, block)]

    def foll_exchange(k):
        dy, dz = SOURCES[k]
        chip = lax.rem(y_hi + dy, 2) * 4 + lax.rem(z + 4 - dz, 4)
        src = foll_ref.at[:, pl.ds(pl.multiple_of(chip * 128, 128), 128)]
        return remote(
            src, foll_rows(2 * k), fo_send.at[2 * k], fo_recv.at[2 * k],
            {"req": req_at(dy, -dz, 0)},
        )

    def foll_sibling(k):
        j = 2 * k + 1
        return remote(
            foll_rows(2 * k), foll_rows(j), fo_send.at[j], fo_recv.at[j], {"req": req_at(0, 0, 1)}
        )

    def lanes(f):
        return pl.ds(PARTS[f][0], PARTS[f][1])

    def sum_first(f, i):
        if i:
            src = part.at[:, lax.rem(x + i, 4), :, lanes(f)]
            return remote(
                src, first_x.at[i - 1, :, :, lanes(f)], s1_send.at[f, i], s1_recv.at[f, i], tp_x(i)
            )
        src = part.at[other, :, :, lanes(f)]
        return remote(src, first_y.at[:, :, lanes(f)], s1_send.at[f, 0], s1_recv.at[f, 0], tp_y)

    def sum_direct(f, i):
        row, column = (y_lo, other)[i // 4], lax.rem(x + i, 4)
        src, dst = part.at[row, column, :, lanes(f)], direct.at[i - 1, :, lanes(f)]
        return remote(src, dst, d1_send.at[f, i], d1_recv.at[f, i], tp_at(i))

    def grad_direct(f, i):
        mine = grad.at[y_lo, x, :, lanes(f)]
        return remote(mine, mine, d2_send.at[f, i], d2_recv.at[f, i], tp_at(i))

    def grad_direct_wait(f, i):
        theirs = grad.at[(y_lo, other)[i // 4], lax.rem(x + 8 - i, 4), :, lanes(f)]
        remote(theirs, theirs, d2_send.at[f, i], d2_recv.at[f, i], tp_at(i)).wait_recv()

    def tp_at(i):
        return {"tp": (y_lo, other)[i // 4] * 4 + lax.rem(x + i, 4)}

    def is_direct(f):
        return PARTS[f][2] == "d"

    def sum_second(f, i):
        slot = (i - 1) % 4
        src, dst = half.at[slot, :, lanes(f)], second.at[slot, :, lanes(f)]
        device = tp_x(i) if i else tp_y
        return remote(src, dst, s2_send.at[f, i], s2_recv.at[f, i], device)

    def grad_first(f, i):
        mine = grad.at[y_lo, x, :, lanes(f)]
        return remote(mine, mine, a1_send.at[f, i], a1_recv.at[f, i], tp_x(i) if i else tp_y)

    def grad_first_wait(f, i):
        theirs = grad.at[y_lo, lax.rem(x + 4 - i, 4), :, lanes(f)] if i else grad.at[
            other, x, :, lanes(f)
        ]
        remote(
            theirs, theirs, a1_send.at[f, i], a1_recv.at[f, i], tp_x(i) if i else tp_y
        ).wait_recv()

    def grad_second(f, i):
        if PARTS[f][2] == "x":
            mine, device = grad.at[other, x, :, lanes(f)], tp_x(i)
        else:
            mine, device = grad.at[y_lo, lax.rem(x + 4 - i, 4), :, lanes(f)], tp_y
        return remote(mine, mine, a2_send.at[f, i], a2_recv.at[f, i], device)

    def grad_second_wait(f, i):
        theirs = grad.at[other, lax.rem(x + 4 - i, 4), :, lanes(f)]
        remote(theirs, theirs, a2_send.at[f, i], a2_recv.at[f, i], tp_y).wait_recv()

    def draft(c):
        parts = CHUNKS[c][1]
        start, stop = parts[0][0], parts[-1][0] + parts[-1][1]
        while start < stop:
            step = min(256, stop - start)
            value = lax.dot_general(
                w_buf[...], hid[pl.ds(start, step), :], (((1,), (1,)), ((), ())),
                preferred_element_type=jnp.float32,
            )
            part[:, :, :, pl.ds(start, step)] = value.astype(jnp.bfloat16).reshape(
                part.shape[:3] + (step,)
            )
            start += step

    def peers(f, stage):
        if is_direct(f):
            return ()
        return (1, 2, 3) if (PARTS[f][2] == "x") == (stage == 0) else (0,)

    def parts_of(c):
        return [f for f in range(len(PARTS)) if PARTS[f] in CHUNKS[c][1]]

    def start_first(c):
        draft(c)
        for f in parts_of(c):
            for i in peers(f, 0):
                sum_first(f, i).start()
            if is_direct(f):
                for i in DIRECT:
                    sum_direct(f, i).start()

    def start_second(c):
        for f in parts_of(c):
            n = lanes(f)
            if is_direct(f):
                continue
            for i in peers(f, 0):
                sum_first(f, i).wait_recv()
            if PARTS[f][2] == "x":

                def summed(g):
                    value = part[g, x, :, n].astype(jnp.float32)
                    for i in range(3):
                        value = value + first_x[i, g, :, n].astype(jnp.float32)
                    return value

                half[3, :, n] = summed(other).astype(jnp.bfloat16)
                sum_second(f, 0).start()
                own[:, n] = summed(y_lo)
            else:

                def summed(g):
                    return part[y_lo, g, :, n].astype(jnp.float32) + first_y[g, :, n].astype(
                        jnp.float32
                    )

                for i in range(1, 4):
                    half[i - 1, :, n] = summed(lax.rem(x + i, 4)).astype(jnp.bfloat16)
                    sum_second(f, i).start()
                own[:, n] = summed(x)

    def start_grad(c):
        for f in parts_of(c):
            n = lanes(f)
            if is_direct(f):
                value = part[y_lo, x, :, n].astype(jnp.float32)
                for i in DIRECT:
                    sum_direct(f, i).wait_recv()
                    value = value + direct[i - 1, :, n].astype(jnp.float32)
            else:
                value = own[:, n]
            for i in peers(f, 1):
                sum_second(f, i).wait_recv()
                value = value + second[(i - 1) % 4, :, n].astype(jnp.float32)
            value = (value - following[:, n]) / QLEN
            grad[y_lo, x, :, n] = value.astype(jnp.bfloat16)
            if is_direct(f):
                for i in DIRECT:
                    grad_direct(f, i).start()
                continue
            for i in range(4):
                grad_first(f, i).start()

    def forward_grad(c):
        for f in parts_of(c):
            if is_direct(f):
                continue
            if PARTS[f][2] == "x":
                grad_first_wait(f, 0)
                for i in range(1, 4):
                    grad_second(f, i).start()
            else:
                for i in range(1, 4):
                    grad_first_wait(f, i)
                    grad_second(f, i).start()

    def project(c):
        for f in parts_of(c):
            if is_direct(f):
                for i in DIRECT:
                    grad_direct_wait(f, i)
                continue
            if PARTS[f][2] == "x":
                for i in range(1, 4):
                    grad_first_wait(f, i)
            else:
                grad_first_wait(f, 0)
            for i in range(1, 4):
                grad_second_wait(f, i)
        start, rows = span_of(c)
        tile = min(256, features)
        for n in range(features // tile):
            columns = pl.ds(n * tile, tile)
            value = jnp.dot(
                grad[:, :, :, pl.ds(start, rows)].reshape(total.shape[0], rows),
                hid[pl.ds(start, rows), columns],
                preferred_element_type=jnp.float32,
            )
            if c == 0:
                total[:, columns] = value
            else:
                total[:, columns] += value
            if c == len(CHUNKS) - 1:
                out_copy(n).start()

    def span_of(c):
        parts = CHUNKS[c][1]
        return parts[0][0], parts[-1][0] + parts[-1][1] - parts[0][0]

    def out_copy(n):
        tile = min(256, features)
        span = (pl.ds(0, total.shape[0]), pl.ds(n * tile, tile))
        return pltpu.make_async_copy(total.at[span], out_ref.at[span], io_sem.at[3 + n])

    def arrive(c):
        for k in CHUNKS[c][0]:
            sibling(k).wait_recv()

    def following_of(half):
        span = rows_all // 2
        rows = foll[pl.ds(half * span, span), :].astype(jnp.float32).T
        return jnp.where(core == 0, rows[:width], rows[width:])

    arrive(0)
    start_first(0)
    gather(2, 0).wait_recv()
    gather(4, 0).start()
    gather(1, 1).wait_recv()
    gather(4, 1).start()
    gather(2, 1).wait_recv()
    sibling(2).start()
    gather(1, 0).wait_recv()
    sibling(1).start()
    for p in range(2):
        gather(3, p).wait_recv()
        gather(6, p).start()
        gather(5, p).start()
    sibling(3).start()
    start_second(0)
    arrive(1)
    start_first(1)
    for k in range(1, 8):
        foll_exchange(k).start()
    for p in range(2):
        gather(4, p).wait_recv()
    sibling(4).start()
    gather(6, 0).wait_recv()
    gather(7, 0).start()
    gather(5, 1).wait_recv()
    gather(7, 1).start()
    gather(6, 1).wait_recv()
    sibling(6).start()
    gather(5, 0).wait_recv()
    sibling(5).start()
    arrive(2)
    start_first(2)
    start_second(1)
    foll_copy.wait()
    foll_sibling(0).start()
    for k in range(1, 8):
        foll_exchange(k).wait_recv()
        foll_sibling(k).start()
    for p in range(2):
        gather(7, p).wait_recv()
    sibling(7).start()
    for k in range(8):
        foll_sibling(k).wait_recv()
    for h in range(2):
        following[:, pl.ds(h * (rows_all // 2), rows_all // 2)] = following_of(h)
    start_grad(0)
    arrive(3)
    start_first(3)
    start_grad(1)
    start_second(2)
    forward_grad(0)
    start_second(3)
    forward_grad(1)
    start_grad(2)
    start_grad(3)
    forward_grad(2)
    forward_grad(3)
    for c in range(len(CHUNKS)):
        project(c)

    for k in range(1, 8):
        for p in range(2):
            gather(k, p).wait_send()
    for k in range(8):
        sibling(k).wait_send()
    for k in range(8):
        if k:
            foll_exchange(k).wait_send()
        foll_sibling(k).wait_send()
    for f in range(len(PARTS)):
        if is_direct(f):
            for i in DIRECT:
                sum_direct(f, i).wait_send()
                grad_direct(f, i).wait_send()
            continue
        for i in peers(f, 0):
            sum_first(f, i).wait_send()
        for i in peers(f, 1):
            sum_second(f, i).wait_send()
        for i in range(4):
            grad_first(f, i).wait_send()
        for i in range(1, 4):
            grad_second(f, i).wait_send()
    for n in range(features // min(256, features)):
        out_copy(n).wait()


def gradient(used, foll, w_flat, n_tp):
    block, features = used.shape
    outs = w_flat.shape[0]
    width = outs // n_tp
    rows = 16 * block
    parts = len(PARTS)
    any_spec = pl.BlockSpec(memory_space=pl.ANY)
    dma = pltpu.SemaphoreType.DMA
    return pl.pallas_call(
        gradient_kernel,
        out_shape=jax.ShapeDtypeStruct((outs, features), jnp.float32),
        in_specs=[any_spec] * 3,
        out_specs=any_spec,
        scratch_shapes=[
            pltpu.VMEM((rows, features), jnp.bfloat16),
            pltpu.VMEM((outs, features), jnp.bfloat16),
            pltpu.VMEM((rows, 128), jnp.bfloat16),
            pltpu.VMEM((width, rows), jnp.float32),
            pltpu.VMEM((2, 4, width, rows), jnp.bfloat16),
            pltpu.VMEM((3, 2, width, rows), jnp.bfloat16),
            pltpu.VMEM((4, width, rows), jnp.bfloat16),
            pltpu.VMEM((4, width, rows), jnp.bfloat16),
            pltpu.VMEM((width, rows), jnp.float32),
            pltpu.VMEM((4, width, rows), jnp.bfloat16),
            pltpu.VMEM((7, width, rows), jnp.bfloat16),
            pltpu.VMEM((2, 4, width, rows), jnp.bfloat16),
            pltpu.VMEM((outs, features), jnp.float32),
            dma((7,)), dma((8, 2)), dma((8, 2)), dma((8,)), dma((8,)), dma((16,)), dma((16,)),
            dma((parts, 4)), dma((parts, 4)), dma((parts, 4)), dma((parts, 4)),
            dma((parts, 4)), dma((parts, 4)), dma((parts, 4)), dma((parts, 4)),
            dma((parts, 8)), dma((parts, 8)), dma((parts, 8)), dma((parts, 8)),
        ],
        compiler_params=pltpu.CompilerParams(
            collective_id=0, has_side_effects=True, vmem_limit_bytes=58 * 2**20
        ),
        name="gradient",
    )(used, foll, w_flat)


WRITES = 8


def write_kernel(in_ref, out_ref, buf, sem):
    rows = in_ref.shape[0] // WRITES

    def piece(n, out):
        span = pl.ds(n * rows, rows)
        if out:
            return pltpu.make_async_copy(buf.at[span], out_ref.at[span], sem.at[1, n])
        return pltpu.make_async_copy(in_ref.at[span], buf.at[span], sem.at[0, n])

    for n in range(WRITES):
        piece(n, False).start()
    for n in range(WRITES):
        piece(n, False).wait()
        piece(n, True).start()
    for n in range(WRITES):
        piece(n, True).wait()


def write(grad):
    any_spec = pl.BlockSpec(memory_space=pl.ANY)
    return pl.pallas_call(
        write_kernel,
        out_shape=jax.ShapeDtypeStruct(grad.shape, grad.dtype),
        in_specs=[any_spec],
        out_specs=any_spec,
        scratch_shapes=[pltpu.VMEM(grad.shape, grad.dtype), pltpu.SemaphoreType.DMA((2, WRITES))],
        compiler_params=pltpu.CompilerParams(vmem_limit_bytes=58 * 2**20),
        name="write",
    )(grad)


def shards(query, k_cache, v_cache, ctx_len, residual, accepted, w_draft):
    requests, new_tokens, heads, head_dim = query.shape
    slots = k_cache.shape[2]
    hidden, used, foll = attention(
        query.reshape(requests, new_tokens * heads, head_dim),
        k_cache.reshape(requests, slots, head_dim),
        v_cache.reshape(requests, slots, head_dim),
        ctx_len, residual, accepted,
    )
    features, groups, width = w_draft.shape
    w_flat = w_draft.transpose(1, 2, 0).reshape(groups * width, features)
    grad = write(gradient(used, foll, w_flat, groups))
    return hidden, grad.reshape(groups, width, features).transpose(2, 0, 1)


def solution(mesh):
    placed = (
        P("req", None, "tp", None),
        P("req", "tp", None, None),
        P("req", "tp", None, None),
        P("req"),
        P("req", "tp"),
        P(),
        P("tp", None, "req"),
    )
    return jax.shard_map(
        shards,
        mesh=mesh,
        in_specs=placed,
        out_specs=(P("req", "tp"), P("tp", None, "req")),
        check_vma=False,
    )
```

```python
import jax
import jax.numpy as jnp
from jax import lax
from jax.experimental import pallas as pl
from jax.experimental.pallas import tpu as pltpu
from jax.sharding import PartitionSpec as P

QLEN = 6
LOG2_E = 1.4426950408889634
GROUP = 8
USED_PER_BLOCK = 80
SHORT = 256
BATCH = 16

MESH = pl.DeviceIdType.MESH


def attend(queries, keys, values, length, scale):
    slots = keys.shape[0]
    scores = lax.dot_general(
        queries, keys, (((1,), (1,)), ((), ())), preferred_element_type=jnp.float32
    ) * (scale * LOG2_E)
    rows, features = queries.shape
    position = lax.broadcasted_iota(jnp.int32, (rows, slots), 1)
    verified = lax.broadcasted_iota(jnp.int32, (rows, slots), 0) // GROUP
    scores = jnp.where(position < verified + (length - QLEN + 1), scores, -jnp.inf)
    top = jnp.max(scores, axis=-1, keepdims=True)
    weights = jnp.exp2(scores - top).astype(jnp.bfloat16)
    values = jnp.concatenate([values, jnp.ones((slots, features), jnp.bfloat16)], axis=1)
    mixed = jnp.dot(weights, values, preferred_element_type=jnp.float32)
    return mixed[:, :features] / mixed[:, features:]


def attention_kernel(
    ctx_ref, accepted_ref, q_hbm, k_hbm, v_hbm, res_hbm,
    hidden_hbm, used_ref, foll_ref,
    q_buf, k_buf, v_buf, res_buf, att_buf, hid_buf, pick_buf, k_sem, v_sem, k_more, v_more, io_sem,
):
    requests, slots, head_dim = k_hbm.shape
    rows = q_buf.shape[1]
    scale = head_dim ** (-0.5)
    batches = requests // BATCH
    all_rows = requests * QLEN
    q_copy = pltpu.make_async_copy(q_hbm, q_buf, io_sem.at[0])
    res_copy = pltpu.make_async_copy(res_hbm, res_buf, io_sem.at[1])
    q_copy.start()

    def short_copies(b):
        span = (pl.ds(b * BATCH, BATCH), pl.ds(0, SHORT))
        return (
            pltpu.make_async_copy(k_hbm.at[span], k_buf.at[span], k_sem.at[b]),
            pltpu.make_async_copy(v_hbm.at[span], v_buf.at[span], v_sem.at[b]),
        )

    def more_copies(r):
        span = (r, pl.ds(SHORT, slots - SHORT))
        return (
            pltpu.make_async_copy(k_hbm.at[span], k_buf.at[span], k_more.at[r]),
            pltpu.make_async_copy(v_hbm.at[span], v_buf.at[span], v_more.at[r]),
        )

    for b in range(batches):
        for copy in short_copies(b):
            copy.start()
    res_copy.start()

    @pl.loop(0, requests)
    def _(r):
        @pl.when(ctx_ref[r] > SHORT)
        def _():
            for copy in more_copies(r):
                copy.start()

    row = lax.broadcasted_iota(jnp.int32, (1, all_rows), 1)
    request = row // QLEN
    verified = row - request * QLEN
    base = lax.axis_index("req") * requests
    place = jnp.full((1, all_rows), -1, jnp.int32)
    next_place = place
    before = jnp.int32(0)
    for r in range(requests):
        count = accepted_ref[base + r]
        mine = request == r
        place = jnp.where(mine & (verified < count), before + verified, place)
        next_place = jnp.where(
            mine & (verified >= 1) & (verified <= count), before + verified - 1, next_place
        )
        before = before + count
    want = lax.broadcasted_iota(jnp.int32, (used_ref.shape[0], all_rows), 0)
    pick_buf[0] = (want == place).astype(jnp.float32).astype(jnp.bfloat16)
    pick_buf[1] = (want == next_place).astype(jnp.float32).astype(jnp.bfloat16)

    q_copy.wait()

    @pl.loop(0, batches)
    def _(b):
        for copy in short_copies(b):
            copy.wait()
        for j in range(BATCH):
            r = b * BATCH + j
            att_buf[pl.ds(pl.multiple_of(r * rows, rows), rows), :] = attend(
                q_buf[r], k_buf[r, 0:SHORT], v_buf[r, 0:SHORT], ctx_ref[r], scale
            )

    @pl.loop(0, requests)
    def _(r):
        @pl.when(ctx_ref[r] > SHORT)
        def _():
            for copy in more_copies(r):
                copy.wait()
            att_buf[pl.ds(pl.multiple_of(r * rows, rows), rows), :] = attend(
                q_buf[r], k_buf[r], v_buf[r], ctx_ref[r], scale
            )

    res_copy.wait()
    for h in range(GROUP):
        columns = pl.ds(h * head_dim, head_dim)
        mixed = att_buf[pl.ds(h, all_rows, stride=GROUP), :]
        hid_buf[:, columns] = (res_buf[:, columns].astype(jnp.float32) + mixed).astype(jnp.bfloat16)
    hidden_copy = pltpu.make_async_copy(hid_buf, hidden_hbm, io_sem.at[2])
    hidden_copy.start()

    hidden = hid_buf[...]
    used_ref[...] = jnp.dot(pick_buf[0], hidden, preferred_element_type=jnp.float32).astype(jnp.bfloat16)
    foll_ref[...] = jnp.dot(pick_buf[1], hidden, preferred_element_type=jnp.float32).astype(jnp.bfloat16)
    hidden_copy.wait()


def attention(query, k_cache, v_cache, ctx_len, residual, accepted):
    requests, slots, head_dim = k_cache.shape
    rows = query.shape[1]
    all_rows, features = residual.shape
    hbm = pl.BlockSpec(memory_space=pl.ANY)
    smem = pl.BlockSpec(memory_space=pltpu.SMEM)
    vmem = pl.BlockSpec(memory_space=pltpu.VMEM)
    batches = requests // BATCH
    return pl.pallas_call(
        attention_kernel,
        out_shape=(
            jax.ShapeDtypeStruct((all_rows, features), jnp.bfloat16),
            jax.ShapeDtypeStruct((USED_PER_BLOCK, features), jnp.bfloat16),
            jax.ShapeDtypeStruct((USED_PER_BLOCK, features), jnp.bfloat16),
        ),
        in_specs=[smem, smem, hbm, hbm, hbm, hbm],
        out_specs=(hbm, vmem, vmem),
        scratch_shapes=[
            pltpu.VMEM((requests, rows, head_dim), jnp.bfloat16),
            pltpu.VMEM((requests, slots, head_dim), jnp.bfloat16),
            pltpu.VMEM((requests, slots, head_dim), jnp.bfloat16),
            pltpu.VMEM((all_rows, features), jnp.bfloat16),
            pltpu.VMEM((requests * rows + GROUP, head_dim), jnp.float32),
            pltpu.VMEM((all_rows, features), jnp.bfloat16),
            pltpu.VMEM((2, USED_PER_BLOCK, all_rows), jnp.bfloat16),
            pltpu.SemaphoreType.DMA((batches,)),
            pltpu.SemaphoreType.DMA((batches,)),
            pltpu.SemaphoreType.DMA((requests,)),
            pltpu.SemaphoreType.DMA((requests,)),
            pltpu.SemaphoreType.DMA((3,)),
        ],
        compiler_params=pltpu.CompilerParams(vmem_limit_bytes=58 * 2**20),
        name="attention",
    )(ctx_len, accepted, query, k_cache, v_cache, residual)


SOURCES = ((0, 0), (0, 1), (0, 3), (1, 0), (0, 2), (1, 1), (1, 3), (1, 2))
CHUNKS = (
    ((0,), ((0, 128, "x"),)),
    ((1, 2, 3), ((128, 256, "x"), (384, 256, "y"))),
    ((4, 5, 6), ((640, 256, "x"), (896, 128, "y"))),
    ((7,), ((1024, 128, "x"), (1152, 128, "y"))),
)
PIECES = ((0, 48), (48, 32))
PARTS = tuple(part for _, parts in CHUNKS for part in parts)
DIRECT = (2, 6, 4, 5, 7, 1, 3)


def gradient_kernel(
    used_ref, foll_ref, w_ref, out_ref,
    hid, w_buf, foll, following, part, first_x, first_y, half, own, second, direct, grad, total,
    io_sem, g_send, g_recv, sib_send, sib_recv, fo_send, fo_recv,
    s1_send, s1_recv, s2_send, s2_recv, a1_send, a1_recv, a2_send, a2_recv,
    d1_send, d1_recv, d2_send, d2_recv,
):
    r = lax.axis_index("req")
    t = lax.axis_index("tp")
    core = lax.rem(r, 2)
    z = lax.rem(r // 2, 4)
    y_hi = r // 8
    x = lax.rem(t, 4)
    y_lo = t // 4
    other = 1 - y_lo
    block, features = used_ref.shape
    width = part.shape[2]
    rows_all = hid.shape[0]

    def req_at(dy, dz, dc):
        return (lax.rem(y_hi + dy, 2) * 4 + lax.rem(z + 4 + dz, 4)) * 2 + lax.rem(core + dc, 2)

    def tp_x(i):
        return {"tp": y_lo * 4 + lax.rem(x + i, 4)}

    tp_y = {"tp": other * 4 + x}

    def tp_diagonal(i):
        return {"tp": other * 4 + lax.rem(x + i, 4)}

    def remote(src, dst, send, recv, device):
        return pltpu.make_async_remote_copy(
            src_ref=src, dst_ref=dst, send_sem=send, recv_sem=recv,
            device_id=device, device_id_type=MESH,
        )

    w_copy = pltpu.make_async_copy(w_ref, w_buf, io_sem.at[0])
    own_copy = pltpu.make_async_copy(used_ref, hid.at[pl.ds(0, block)], io_sem.at[1])
    foll_copy = pltpu.make_async_copy(
        foll_ref.at[:, pl.ds(pl.multiple_of(r // 2 * 128, 128), 128)],
        foll.at[pl.ds(0, block)],
        io_sem.at[2],
    )
    own_copy.start()
    w_copy.start()
    foll_copy.start()

    barrier = pltpu.get_barrier_semaphore()
    for dy, dz in SOURCES:
        dc = int((dy, dz) == (0, 0))
        pl.semaphore_signal(
            barrier, inc=1, device_id={"req": req_at(dy, dz, dc)}, device_id_type=MESH
        )
    for i in range(1, 4):
        pl.semaphore_signal(barrier, inc=1, device_id=tp_x(i), device_id_type=MESH)
        pl.semaphore_signal(barrier, inc=1, device_id=tp_diagonal(i), device_id_type=MESH)
    pl.semaphore_signal(barrier, inc=1, device_id=tp_y, device_id_type=MESH)
    pl.semaphore_wait(barrier, 15)

    up, down, across = (0, 1), (0, -1), (1, 0)
    routes = {
        1: ((0, down), (0, down)), 2: ((0, up), (0, up)), 3: ((0, across), (0, across)),
        4: ((2, up), (1, down)), 5: ((3, down), (3, down)), 6: ((3, up), (3, up)),
        7: ((6, up), (5, down)),
    }

    def shard(k, p):
        start, rows = PIECES[p]
        return hid.at[pl.ds(2 * block * k + start, rows)]

    def gather(k, p):
        source, target = routes[k][p]
        start, rows = PIECES[p]
        return remote(
            shard(source, p) if source else used_ref.at[pl.ds(start, rows)], shard(k, p),
            g_send.at[k, p], g_recv.at[k, p], {"req": req_at(*target, 0)},
        )

    def sibling(k):
        src = used_ref if k == 0 else hid.at[pl.ds(2 * block * k, block)]
        dst = hid.at[pl.ds(2 * block * k + block, block)]
        return remote(src, dst, sib_send.at[k], sib_recv.at[k], {"req": req_at(0, 0, 1)})

    for p in range(2):
        gather(2, p).start()
        gather(1, 1 - p).start()
        gather(3, p).start()
    sibling(0).start()

    own_copy.wait()
    w_copy.wait()

    def foll_rows(j):
        return foll.at[pl.ds(j * block, block)]

    def foll_exchange(k):
        dy, dz = SOURCES[k]
        chip = lax.rem(y_hi + dy, 2) * 4 + lax.rem(z + 4 - dz, 4)
        src = foll_ref.at[:, pl.ds(pl.multiple_of(chip * 128, 128), 128)]
        return remote(
            src, foll_rows(2 * k), fo_send.at[2 * k], fo_recv.at[2 * k],
            {"req": req_at(dy, -dz, 0)},
        )

    def foll_sibling(k):
        j = 2 * k + 1
        return remote(
            foll_rows(2 * k), foll_rows(j), fo_send.at[j], fo_recv.at[j], {"req": req_at(0, 0, 1)}
        )

    def lanes(f):
        return pl.ds(PARTS[f][0], PARTS[f][1])

    def sum_first(f, i):
        if i:
            src = part.at[:, lax.rem(x + i, 4), :, lanes(f)]
            return remote(
                src, first_x.at[i - 1, :, :, lanes(f)], s1_send.at[f, i], s1_recv.at[f, i], tp_x(i)
            )
        src = part.at[other, :, :, lanes(f)]
        return remote(src, first_y.at[:, :, lanes(f)], s1_send.at[f, 0], s1_recv.at[f, 0], tp_y)

    def sum_direct(f, i):
        row, column = (y_lo, other)[i // 4], lax.rem(x + i, 4)
        src, dst = part.at[row, column, :, lanes(f)], direct.at[i - 1, :, lanes(f)]
        return remote(src, dst, d1_send.at[f, i], d1_recv.at[f, i], tp_at(i))

    def grad_direct(f, i):
        mine = grad.at[y_lo, x, :, lanes(f)]
        return remote(mine, mine, d2_send.at[f, i], d2_recv.at[f, i], tp_at(i))

    def grad_direct_wait(f, i):
        theirs = grad.at[(y_lo, other)[i // 4], lax.rem(x + 8 - i, 4), :, lanes(f)]
        remote(theirs, theirs, d2_send.at[f, i], d2_recv.at[f, i], tp_at(i)).wait_recv()

    def tp_at(i):
        return {"tp": (y_lo, other)[i // 4] * 4 + lax.rem(x + i, 4)}

    def is_direct(f):
        return PARTS[f][2] == "d"

    def sum_second(f, i):
        slot = (i - 1) % 4
        src, dst = half.at[slot, :, lanes(f)], second.at[slot, :, lanes(f)]
        device = tp_x(i) if i else tp_y
        return remote(src, dst, s2_send.at[f, i], s2_recv.at[f, i], device)

    def grad_first(f, i):
        mine = grad.at[y_lo, x, :, lanes(f)]
        return remote(mine, mine, a1_send.at[f, i], a1_recv.at[f, i], tp_x(i) if i else tp_y)

    def grad_first_wait(f, i):
        theirs = grad.at[y_lo, lax.rem(x + 4 - i, 4), :, lanes(f)] if i else grad.at[
            other, x, :, lanes(f)
        ]
        remote(
            theirs, theirs, a1_send.at[f, i], a1_recv.at[f, i], tp_x(i) if i else tp_y
        ).wait_recv()

    def grad_second(f, i):
        if PARTS[f][2] == "x":
            mine, device = grad.at[other, x, :, lanes(f)], tp_x(i)
        else:
            mine, device = grad.at[y_lo, lax.rem(x + 4 - i, 4), :, lanes(f)], tp_y
        return remote(mine, mine, a2_send.at[f, i], a2_recv.at[f, i], device)

    def grad_second_wait(f, i):
        theirs = grad.at[other, lax.rem(x + 4 - i, 4), :, lanes(f)]
        remote(theirs, theirs, a2_send.at[f, i], a2_recv.at[f, i], tp_y).wait_recv()

    def draft(c):
        parts = CHUNKS[c][1]
        start, stop = parts[0][0], parts[-1][0] + parts[-1][1]
        while start < stop:
            step = min(256, stop - start)
            value = lax.dot_general(
                w_buf[...], hid[pl.ds(start, step), :], (((1,), (1,)), ((), ())),
                preferred_element_type=jnp.float32,
            )
            part[:, :, :, pl.ds(start, step)] = value.astype(jnp.bfloat16).reshape(
                part.shape[:3] + (step,)
            )
            start += step

    def peers(f, stage):
        if is_direct(f):
            return ()
        return (1, 2, 3) if (PARTS[f][2] == "x") == (stage == 0) else (0,)

    def parts_of(c):
        return [f for f in range(len(PARTS)) if PARTS[f] in CHUNKS[c][1]]

    def start_first(c):
        draft(c)
        for f in parts_of(c):
            for i in peers(f, 0):
                sum_first(f, i).start()
            if is_direct(f):
                for i in DIRECT:
                    sum_direct(f, i).start()

    def start_second(c):
        for f in parts_of(c):
            n = lanes(f)
            if is_direct(f):
                continue
            for i in peers(f, 0):
                sum_first(f, i).wait_recv()
            if PARTS[f][2] == "x":

                def summed(g):
                    value = part[g, x, :, n].astype(jnp.float32)
                    for i in range(3):
                        value = value + first_x[i, g, :, n].astype(jnp.float32)
                    return value

                half[3, :, n] = summed(other).astype(jnp.bfloat16)
                sum_second(f, 0).start()
                own[:, n] = summed(y_lo)
            else:

                def summed(g):
                    return part[y_lo, g, :, n].astype(jnp.float32) + first_y[g, :, n].astype(
                        jnp.float32
                    )

                for i in range(1, 4):
                    half[i - 1, :, n] = summed(lax.rem(x + i, 4)).astype(jnp.bfloat16)
                    sum_second(f, i).start()
                own[:, n] = summed(x)

    def start_grad(c):
        for f in parts_of(c):
            n = lanes(f)
            if is_direct(f):
                value = part[y_lo, x, :, n].astype(jnp.float32)
                for i in DIRECT:
                    sum_direct(f, i).wait_recv()
                    value = value + direct[i - 1, :, n].astype(jnp.float32)
            else:
                value = own[:, n]
            for i in peers(f, 1):
                sum_second(f, i).wait_recv()
                value = value + second[(i - 1) % 4, :, n].astype(jnp.float32)
            value = (value - following[:, n]) / QLEN
            grad[y_lo, x, :, n] = value.astype(jnp.bfloat16)
            if is_direct(f):
                for i in DIRECT:
                    grad_direct(f, i).start()
                continue
            for i in range(4):
                grad_first(f, i).start()

    def forward_grad(c):
        for f in parts_of(c):
            if is_direct(f):
                continue
            if PARTS[f][2] == "x":
                grad_first_wait(f, 0)
                for i in range(1, 4):
                    grad_second(f, i).start()
            else:
                for i in range(1, 4):
                    grad_first_wait(f, i)
                    grad_second(f, i).start()

    def project(c):
        for f in parts_of(c):
            if is_direct(f):
                for i in DIRECT:
                    grad_direct_wait(f, i)
                continue
            if PARTS[f][2] == "x":
                for i in range(1, 4):
                    grad_first_wait(f, i)
            else:
                grad_first_wait(f, 0)
            for i in range(1, 4):
                grad_second_wait(f, i)
        start, rows = span_of(c)
        tile = min(256, features)
        for n in range(features // tile):
            columns = pl.ds(n * tile, tile)
            value = jnp.dot(
                grad[:, :, :, pl.ds(start, rows)].reshape(total.shape[0], rows),
                hid[pl.ds(start, rows), columns],
                preferred_element_type=jnp.float32,
            )
            if c == 0:
                total[:, columns] = value
            else:
                total[:, columns] += value
            if c == len(CHUNKS) - 1:
                out_copy(n).start()

    def span_of(c):
        parts = CHUNKS[c][1]
        return parts[0][0], parts[-1][0] + parts[-1][1] - parts[0][0]

    def out_copy(n):
        tile = min(256, features)
        span = (pl.ds(0, total.shape[0]), pl.ds(n * tile, tile))
        return pltpu.make_async_copy(total.at[span], out_ref.at[span], io_sem.at[3 + n])

    def arrive(c):
        for k in CHUNKS[c][0]:
            sibling(k).wait_recv()

    def following_of(half):
        span = rows_all // 2
        rows = foll[pl.ds(half * span, span), :].astype(jnp.float32).T
        return jnp.where(core == 0, rows[:width], rows[width:])

    arrive(0)
    start_first(0)
    gather(2, 0).wait_recv()
    gather(4, 0).start()
    gather(1, 1).wait_recv()
    gather(4, 1).start()
    gather(2, 1).wait_recv()
    sibling(2).start()
    gather(1, 0).wait_recv()
    sibling(1).start()
    for p in range(2):
        gather(3, p).wait_recv()
        gather(6, p).start()
        gather(5, p).start()
    sibling(3).start()
    start_second(0)
    arrive(1)
    start_first(1)
    for k in range(1, 8):
        foll_exchange(k).start()
    for p in range(2):
        gather(4, p).wait_recv()
    sibling(4).start()
    gather(6, 0).wait_recv()
    gather(7, 0).start()
    gather(5, 1).wait_recv()
    gather(7, 1).start()
    gather(6, 1).wait_recv()
    sibling(6).start()
    gather(5, 0).wait_recv()
    sibling(5).start()
    arrive(2)
    start_first(2)
    start_second(1)
    foll_copy.wait()
    foll_sibling(0).start()
    for k in range(1, 8):
        foll_exchange(k).wait_recv()
        foll_sibling(k).start()
    for p in range(2):
        gather(7, p).wait_recv()
    sibling(7).start()
    for k in range(8):
        foll_sibling(k).wait_recv()
    for h in range(2):
        following[:, pl.ds(h * (rows_all // 2), rows_all // 2)] = following_of(h)
    start_grad(0)
    arrive(3)
    start_first(3)
    start_grad(1)
    start_second(2)
    forward_grad(0)
    start_second(3)
    forward_grad(1)
    start_grad(2)
    start_grad(3)
    forward_grad(2)
    forward_grad(3)
    for c in range(len(CHUNKS)):
        project(c)

    for k in range(1, 8):
        for p in range(2):
            gather(k, p).wait_send()
    for k in range(8):
        sibling(k).wait_send()
    for k in range(8):
        if k:
            foll_exchange(k).wait_send()
        foll_sibling(k).wait_send()
    for f in range(len(PARTS)):
        if is_direct(f):
            for i in DIRECT:
                sum_direct(f, i).wait_send()
                grad_direct(f, i).wait_send()
            continue
        for i in peers(f, 0):
            sum_first(f, i).wait_send()
        for i in peers(f, 1):
            sum_second(f, i).wait_send()
        for i in range(4):
            grad_first(f, i).wait_send()
        for i in range(1, 4):
            grad_second(f, i).wait_send()
    for n in range(features // min(256, features)):
        out_copy(n).wait()


def gradient(used, foll, w_flat, n_tp):
    block, features = used.shape
    outs = w_flat.shape[0]
    width = outs // n_tp
    rows = 16 * block
    parts = len(PARTS)
    any_spec = pl.BlockSpec(memory_space=pl.ANY)
    dma = pltpu.SemaphoreType.DMA
    return pl.pallas_call(
        gradient_kernel,
        out_shape=jax.ShapeDtypeStruct((outs, features), jnp.float32),
        in_specs=[any_spec] * 3,
        out_specs=any_spec,
        scratch_shapes=[
            pltpu.VMEM((rows, features), jnp.bfloat16),
            pltpu.VMEM((outs, features), jnp.bfloat16),
            pltpu.VMEM((rows, 128), jnp.bfloat16),
            pltpu.VMEM((width, rows), jnp.float32),
            pltpu.VMEM((2, 4, width, rows), jnp.bfloat16),
            pltpu.VMEM((3, 2, width, rows), jnp.bfloat16),
            pltpu.VMEM((4, width, rows), jnp.bfloat16),
            pltpu.VMEM((4, width, rows), jnp.bfloat16),
            pltpu.VMEM((width, rows), jnp.float32),
            pltpu.VMEM((4, width, rows), jnp.bfloat16),
            pltpu.VMEM((7, width, rows), jnp.bfloat16),
            pltpu.VMEM((2, 4, width, rows), jnp.bfloat16),
            pltpu.VMEM((outs, features), jnp.float32),
            dma((7,)), dma((8, 2)), dma((8, 2)), dma((8,)), dma((8,)), dma((16,)), dma((16,)),
            dma((parts, 4)), dma((parts, 4)), dma((parts, 4)), dma((parts, 4)),
            dma((parts, 4)), dma((parts, 4)), dma((parts, 4)), dma((parts, 4)),
            dma((parts, 8)), dma((parts, 8)), dma((parts, 8)), dma((parts, 8)),
        ],
        compiler_params=pltpu.CompilerParams(
            collective_id=0, has_side_effects=True, vmem_limit_bytes=58 * 2**20
        ),
        name="gradient",
    )(used, foll, w_flat)


WRITES = 8


def write_kernel(in_ref, out_ref, buf, sem):
    rows = in_ref.shape[0] // WRITES

    def piece(n, out):
        span = pl.ds(n * rows, rows)
        if out:
            return pltpu.make_async_copy(buf.at[span], out_ref.at[span], sem.at[1, n])
        return pltpu.make_async_copy(in_ref.at[span], buf.at[span], sem.at[0, n])

    for n in range(WRITES):
        piece(n, False).start()
    for n in range(WRITES):
        piece(n, False).wait()
        piece(n, True).start()
    for n in range(WRITES):
        piece(n, True).wait()


def write(grad):
    any_spec = pl.BlockSpec(memory_space=pl.ANY)
    return pl.pallas_call(
        write_kernel,
        out_shape=jax.ShapeDtypeStruct(grad.shape, grad.dtype),
        in_specs=[any_spec],
        out_specs=any_spec,
        scratch_shapes=[pltpu.VMEM(grad.shape, grad.dtype), pltpu.SemaphoreType.DMA((2, WRITES))],
        compiler_params=pltpu.CompilerParams(vmem_limit_bytes=58 * 2**20),
        name="write",
    )(grad)


def shards(query, k_cache, v_cache, ctx_len, residual, accepted, w_draft):
    requests, new_tokens, heads, head_dim = query.shape
    slots = k_cache.shape[2]
    hidden, used, foll = attention(
        query.reshape(requests, new_tokens * heads, head_dim),
        k_cache.reshape(requests, slots, head_dim),
        v_cache.reshape(requests, slots, head_dim),
        ctx_len, residual, accepted,
    )
    features, groups, width = w_draft.shape
    w_flat = w_draft.transpose(1, 2, 0).reshape(groups * width, features)
    grad = write(gradient(used, foll, w_flat, groups))
    return hidden, grad.reshape(groups, width, features).transpose(2, 0, 1)


def solution(mesh):
    placed = (
        P("req", None, "tp", None),
        P("req", "tp", None, None),
        P("req", "tp", None, None),
        P("req"),
        P("req", "tp"),
        P(),
        P("tp", None, "req"),
    )
    return jax.shard_map(
        shards,
        mesh=mesh,
        in_specs=placed,
        out_specs=(P("req", "tp"), P("tp", None, "req")),
        check_vma=False,
    )
```

```python
import jax
import jax.numpy as jnp
from jax import lax
from jax.experimental import pallas as pl
from jax.experimental.pallas import tpu as pltpu
from jax.sharding import PartitionSpec as P

QLEN = 6
LOG2_E = 1.4426950408889634
GROUP = 8
USED_PER_BLOCK = 80
SHORT = 256
BATCH = 16

MESH = pl.DeviceIdType.MESH


def attend(queries, keys, values, length, scale):
    slots = keys.shape[0]
    scores = lax.dot_general(
        queries, keys, (((1,), (1,)), ((), ())), preferred_element_type=jnp.float32
    ) * (scale * LOG2_E)
    rows, features = queries.shape
    position = lax.broadcasted_iota(jnp.int32, (rows, slots), 1)
    verified = lax.broadcasted_iota(jnp.int32, (rows, slots), 0) // GROUP
    scores = jnp.where(position < verified + (length - QLEN + 1), scores, -jnp.inf)
    top = jnp.max(scores, axis=-1, keepdims=True)
    weights = jnp.exp2(scores - top).astype(jnp.bfloat16)
    values = jnp.concatenate([values, jnp.ones((slots, features), jnp.bfloat16)], axis=1)
    mixed = jnp.dot(weights, values, preferred_element_type=jnp.float32)
    return mixed[:, :features] / mixed[:, features:]


def attention_kernel(
    ctx_ref, accepted_ref, q_hbm, k_hbm, v_hbm, res_hbm,
    hidden_hbm, used_hbm, foll_hbm,
    q_buf, k_buf, v_buf, res_buf, att_buf, hid_buf, pick_buf, rows_buf, k_sem, v_sem, k_more, v_more, io_sem,
):
    requests, slots, head_dim = k_hbm.shape
    rows = q_buf.shape[1]
    scale = head_dim ** (-0.5)
    batches = requests // BATCH
    all_rows = requests * QLEN
    q_copy = pltpu.make_async_copy(q_hbm, q_buf, io_sem.at[0])
    res_copy = pltpu.make_async_copy(res_hbm, res_buf, io_sem.at[1])
    q_copy.start()

    def short_copies(b):
        span = (pl.ds(b * BATCH, BATCH), pl.ds(0, SHORT))
        return (
            pltpu.make_async_copy(k_hbm.at[span], k_buf.at[span], k_sem.at[b]),
            pltpu.make_async_copy(v_hbm.at[span], v_buf.at[span], v_sem.at[b]),
        )

    def more_copies(r):
        span = (r, pl.ds(SHORT, slots - SHORT))
        return (
            pltpu.make_async_copy(k_hbm.at[span], k_buf.at[span], k_more.at[r]),
            pltpu.make_async_copy(v_hbm.at[span], v_buf.at[span], v_more.at[r]),
        )

    for b in range(batches):
        for copy in short_copies(b):
            copy.start()
    res_copy.start()

    @pl.loop(0, requests)
    def _(r):
        @pl.when(ctx_ref[r] > SHORT)
        def _():
            for copy in more_copies(r):
                copy.start()

    row = lax.broadcasted_iota(jnp.int32, (1, all_rows), 1)
    request = row // QLEN
    verified = row - request * QLEN
    base = lax.axis_index("req") * requests
    place = jnp.full((1, all_rows), -1, jnp.int32)
    next_place = place
    before = jnp.int32(0)
    for r in range(requests):
        count = accepted_ref[base + r]
        mine = request == r
        place = jnp.where(mine & (verified < count), before + verified, place)
        next_place = jnp.where(
            mine & (verified >= 1) & (verified <= count), before + verified - 1, next_place
        )
        before = before + count
    want = lax.broadcasted_iota(jnp.int32, (USED_PER_BLOCK, all_rows), 0)
    pick_buf[0] = (want == place).astype(jnp.float32).astype(jnp.bfloat16)
    pick_buf[1] = (want == next_place).astype(jnp.float32).astype(jnp.bfloat16)

    q_copy.wait()

    @pl.loop(0, batches)
    def _(b):
        for copy in short_copies(b):
            copy.wait()
        for j in range(BATCH):
            r = b * BATCH + j
            att_buf[pl.ds(pl.multiple_of(r * rows, rows), rows), :] = attend(
                q_buf[r], k_buf[r, 0:SHORT], v_buf[r, 0:SHORT], ctx_ref[r], scale
            )

    @pl.loop(0, requests)
    def _(r):
        @pl.when(ctx_ref[r] > SHORT)
        def _():
            for copy in more_copies(r):
                copy.wait()
            att_buf[pl.ds(pl.multiple_of(r * rows, rows), rows), :] = attend(
                q_buf[r], k_buf[r], v_buf[r], ctx_ref[r], scale
            )

    res_copy.wait()
    for h in range(GROUP):
        columns = pl.ds(h * head_dim, head_dim)
        mixed = att_buf[pl.ds(h, all_rows, stride=GROUP), :]
        hid_buf[:, columns] = (res_buf[:, columns].astype(jnp.float32) + mixed).astype(jnp.bfloat16)
    hidden_copy = pltpu.make_async_copy(hid_buf, hidden_hbm, io_sem.at[2])
    hidden_copy.start()

    hidden = hid_buf[...]
    copies = [hidden_copy]
    for i, out in enumerate((used_hbm, foll_hbm)):
        rows_buf[i] = jnp.dot(
            pick_buf[i], hidden, preferred_element_type=jnp.float32
        ).astype(jnp.bfloat16)
        copies.append(pltpu.make_async_copy(rows_buf.at[i], out, io_sem.at[3 + i]))
        copies[-1].start()
    for copy in copies:
        copy.wait()


def attention(query, k_cache, v_cache, ctx_len, residual, accepted):
    requests, slots, head_dim = k_cache.shape
    rows = query.shape[1]
    all_rows, features = residual.shape
    hbm = pl.BlockSpec(memory_space=pl.ANY)
    smem = pl.BlockSpec(memory_space=pltpu.SMEM)
    batches = requests // BATCH
    return pl.pallas_call(
        attention_kernel,
        out_shape=(
            jax.ShapeDtypeStruct((all_rows, features), jnp.bfloat16),
            jax.ShapeDtypeStruct((USED_PER_BLOCK, features), jnp.bfloat16),
            jax.ShapeDtypeStruct((USED_PER_BLOCK, features), jnp.bfloat16),
        ),
        in_specs=[smem, smem, hbm, hbm, hbm, hbm],
        out_specs=(hbm, hbm, hbm),
        scratch_shapes=[
            pltpu.VMEM((requests, rows, head_dim), jnp.bfloat16),
            pltpu.VMEM((requests, slots, head_dim), jnp.bfloat16),
            pltpu.VMEM((requests, slots, head_dim), jnp.bfloat16),
            pltpu.VMEM((all_rows, features), jnp.bfloat16),
            pltpu.VMEM((requests * rows + GROUP, head_dim), jnp.float32),
            pltpu.VMEM((all_rows, features), jnp.bfloat16),
            pltpu.VMEM((2, USED_PER_BLOCK, all_rows), jnp.bfloat16),
            pltpu.VMEM((2, USED_PER_BLOCK, features), jnp.bfloat16),
            pltpu.SemaphoreType.DMA((batches,)),
            pltpu.SemaphoreType.DMA((batches,)),
            pltpu.SemaphoreType.DMA((requests,)),
            pltpu.SemaphoreType.DMA((requests,)),
            pltpu.SemaphoreType.DMA((5,)),
        ],
        compiler_params=pltpu.CompilerParams(vmem_limit_bytes=58 * 2**20),
        name="attention",
    )(ctx_len, accepted, query, k_cache, v_cache, residual)


SOURCES = ((0, 0), (0, 1), (0, 3), (1, 0), (0, 2), (1, 1), (1, 3), (1, 2))
CHUNKS = (
    ((0,), ((0, 128, "x"),)),
    ((1, 2, 3), ((128, 256, "x"), (384, 256, "y"))),
    ((4, 5, 6), ((640, 256, "x"), (896, 128, "y"))),
    ((7,), ((1024, 128, "x"), (1152, 128, "y"))),
)
PIECES = ((0, 48), (48, 32))
PARTS = tuple(part for _, parts in CHUNKS for part in parts)
DIRECT = (2, 6, 4, 5, 7, 1, 3)


def gradient_kernel(
    used_ref, foll_ref, w_ref, out_ref,
    hid, w_buf, foll, following, part, first_x, first_y, half, own, second, direct, grad, total,
    io_sem, g_send, g_recv, sib_send, sib_recv, fo_send, fo_recv,
    s1_send, s1_recv, s2_send, s2_recv, a1_send, a1_recv, a2_send, a2_recv,
    d1_send, d1_recv, d2_send, d2_recv,
):
    r = lax.axis_index("req")
    t = lax.axis_index("tp")
    core = lax.rem(r, 2)
    z = lax.rem(r // 2, 4)
    y_hi = r // 8
    x = lax.rem(t, 4)
    y_lo = t // 4
    other = 1 - y_lo
    block, features = used_ref.shape
    width = part.shape[2]
    rows_all = hid.shape[0]

    def req_at(dy, dz, dc):
        return (lax.rem(y_hi + dy, 2) * 4 + lax.rem(z + 4 + dz, 4)) * 2 + lax.rem(core + dc, 2)

    def tp_x(i):
        return {"tp": y_lo * 4 + lax.rem(x + i, 4)}

    tp_y = {"tp": other * 4 + x}

    def tp_diagonal(i):
        return {"tp": other * 4 + lax.rem(x + i, 4)}

    def remote(src, dst, send, recv, device):
        return pltpu.make_async_remote_copy(
            src_ref=src, dst_ref=dst, send_sem=send, recv_sem=recv,
            device_id=device, device_id_type=MESH,
        )

    w_copy = pltpu.make_async_copy(w_ref, w_buf, io_sem.at[0])
    own_copy = pltpu.make_async_copy(used_ref, hid.at[pl.ds(0, block)], io_sem.at[1])
    foll_copy = pltpu.make_async_copy(
        foll_ref.at[:, pl.ds(pl.multiple_of(r // 2 * 128, 128), 128)],
        foll.at[pl.ds(0, block)],
        io_sem.at[2],
    )
    own_copy.start()
    w_copy.start()
    foll_copy.start()

    barrier = pltpu.get_barrier_semaphore()
    for dy, dz in SOURCES:
        dc = int((dy, dz) == (0, 0))
        pl.semaphore_signal(
            barrier, inc=1, device_id={"req": req_at(dy, dz, dc)}, device_id_type=MESH
        )
    for i in range(1, 4):
        pl.semaphore_signal(barrier, inc=1, device_id=tp_x(i), device_id_type=MESH)
        pl.semaphore_signal(barrier, inc=1, device_id=tp_diagonal(i), device_id_type=MESH)
    pl.semaphore_signal(barrier, inc=1, device_id=tp_y, device_id_type=MESH)
    pl.semaphore_wait(barrier, 15)

    up, down, across = (0, 1), (0, -1), (1, 0)
    routes = {
        1: ((0, down), (0, down)), 2: ((0, up), (0, up)), 3: ((0, across), (0, across)),
        4: ((2, up), (1, down)), 5: ((3, down), (3, down)), 6: ((3, up), (3, up)),
        7: ((6, up), (5, down)),
    }

    def shard(k, p):
        start, rows = PIECES[p]
        return hid.at[pl.ds(2 * block * k + start, rows)]

    def gather(k, p):
        source, target = routes[k][p]
        start, rows = PIECES[p]
        return remote(
            shard(source, p) if source else used_ref.at[pl.ds(start, rows)], shard(k, p),
            g_send.at[k, p], g_recv.at[k, p], {"req": req_at(*target, 0)},
        )

    def sibling(k):
        src = used_ref if k == 0 else hid.at[pl.ds(2 * block * k, block)]
        dst = hid.at[pl.ds(2 * block * k + block, block)]
        return remote(src, dst, sib_send.at[k], sib_recv.at[k], {"req": req_at(0, 0, 1)})

    for p in range(2):
        gather(2, p).start()
        gather(1, 1 - p).start()
        gather(3, p).start()
    sibling(0).start()

    own_copy.wait()
    w_copy.wait()

    def foll_rows(j):
        return foll.at[pl.ds(j * block, block)]

    def foll_exchange(k):
        dy, dz = SOURCES[k]
        chip = lax.rem(y_hi + dy, 2) * 4 + lax.rem(z + 4 - dz, 4)
        src = foll_ref.at[:, pl.ds(pl.multiple_of(chip * 128, 128), 128)]
        return remote(
            src, foll_rows(2 * k), fo_send.at[2 * k], fo_recv.at[2 * k],
            {"req": req_at(dy, -dz, 0)},
        )

    def foll_sibling(k):
        j = 2 * k + 1
        return remote(
            foll_rows(2 * k), foll_rows(j), fo_send.at[j], fo_recv.at[j], {"req": req_at(0, 0, 1)}
        )

    def lanes(f):
        return pl.ds(PARTS[f][0], PARTS[f][1])

    def sum_first(f, i):
        if i:
            src = part.at[:, lax.rem(x + i, 4), :, lanes(f)]
            return remote(
                src, first_x.at[i - 1, :, :, lanes(f)], s1_send.at[f, i], s1_recv.at[f, i], tp_x(i)
            )
        src = part.at[other, :, :, lanes(f)]
        return remote(src, first_y.at[:, :, lanes(f)], s1_send.at[f, 0], s1_recv.at[f, 0], tp_y)

    def sum_direct(f, i):
        row, column = (y_lo, other)[i // 4], lax.rem(x + i, 4)
        src, dst = part.at[row, column, :, lanes(f)], direct.at[i - 1, :, lanes(f)]
        return remote(src, dst, d1_send.at[f, i], d1_recv.at[f, i], tp_at(i))

    def grad_direct(f, i):
        mine = grad.at[y_lo, x, :, lanes(f)]
        return remote(mine, mine, d2_send.at[f, i], d2_recv.at[f, i], tp_at(i))

    def grad_direct_wait(f, i):
        theirs = grad.at[(y_lo, other)[i // 4], lax.rem(x + 8 - i, 4), :, lanes(f)]
        remote(theirs, theirs, d2_send.at[f, i], d2_recv.at[f, i], tp_at(i)).wait_recv()

    def tp_at(i):
        return {"tp": (y_lo, other)[i // 4] * 4 + lax.rem(x + i, 4)}

    def is_direct(f):
        return PARTS[f][2] == "d"

    def sum_second(f, i):
        slot = (i - 1) % 4
        src, dst = half.at[slot, :, lanes(f)], second.at[slot, :, lanes(f)]
        device = tp_x(i) if i else tp_y
        return remote(src, dst, s2_send.at[f, i], s2_recv.at[f, i], device)

    def grad_first(f, i):
        mine = grad.at[y_lo, x, :, lanes(f)]
        return remote(mine, mine, a1_send.at[f, i], a1_recv.at[f, i], tp_x(i) if i else tp_y)

    def grad_first_wait(f, i):
        theirs = grad.at[y_lo, lax.rem(x + 4 - i, 4), :, lanes(f)] if i else grad.at[
            other, x, :, lanes(f)
        ]
        remote(
            theirs, theirs, a1_send.at[f, i], a1_recv.at[f, i], tp_x(i) if i else tp_y
        ).wait_recv()

    def grad_second(f, i):
        if PARTS[f][2] == "x":
            mine, device = grad.at[other, x, :, lanes(f)], tp_x(i)
        else:
            mine, device = grad.at[y_lo, lax.rem(x + 4 - i, 4), :, lanes(f)], tp_y
        return remote(mine, mine, a2_send.at[f, i], a2_recv.at[f, i], device)

    def grad_second_wait(f, i):
        theirs = grad.at[other, lax.rem(x + 4 - i, 4), :, lanes(f)]
        remote(theirs, theirs, a2_send.at[f, i], a2_recv.at[f, i], tp_y).wait_recv()

    def draft(c):
        parts = CHUNKS[c][1]
        start, stop = parts[0][0], parts[-1][0] + parts[-1][1]
        while start < stop:
            step = min(256, stop - start)
            value = lax.dot_general(
                w_buf[...], hid[pl.ds(start, step), :], (((1,), (1,)), ((), ())),
                preferred_element_type=jnp.float32,
            )
            part[:, :, :, pl.ds(start, step)] = value.astype(jnp.bfloat16).reshape(
                part.shape[:3] + (step,)
            )
            start += step

    def peers(f, stage):
        if is_direct(f):
            return ()
        return (1, 2, 3) if (PARTS[f][2] == "x") == (stage == 0) else (0,)

    def parts_of(c):
        return [f for f in range(len(PARTS)) if PARTS[f] in CHUNKS[c][1]]

    def start_first(c):
        draft(c)
        for f in parts_of(c):
            for i in peers(f, 0):
                sum_first(f, i).start()
            if is_direct(f):
                for i in DIRECT:
                    sum_direct(f, i).start()

    def start_second(c):
        for f in parts_of(c):
            n = lanes(f)
            if is_direct(f):
                continue
            for i in peers(f, 0):
                sum_first(f, i).wait_recv()
            if PARTS[f][2] == "x":

                def summed(g):
                    value = part[g, x, :, n].astype(jnp.float32)
                    for i in range(3):
                        value = value + first_x[i, g, :, n].astype(jnp.float32)
                    return value

                half[3, :, n] = summed(other).astype(jnp.bfloat16)
                sum_second(f, 0).start()
                own[:, n] = summed(y_lo)
            else:

                def summed(g):
                    return part[y_lo, g, :, n].astype(jnp.float32) + first_y[g, :, n].astype(
                        jnp.float32
                    )

                for i in range(1, 4):
                    half[i - 1, :, n] = summed(lax.rem(x + i, 4)).astype(jnp.bfloat16)
                    sum_second(f, i).start()
                own[:, n] = summed(x)

    def start_grad(c):
        for f in parts_of(c):
            n = lanes(f)
            if is_direct(f):
                value = part[y_lo, x, :, n].astype(jnp.float32)
                for i in DIRECT:
                    sum_direct(f, i).wait_recv()
                    value = value + direct[i - 1, :, n].astype(jnp.float32)
            else:
                value = own[:, n]
            for i in peers(f, 1):
                sum_second(f, i).wait_recv()
                value = value + second[(i - 1) % 4, :, n].astype(jnp.float32)
            value = (value - following[:, n]) / QLEN
            grad[y_lo, x, :, n] = value.astype(jnp.bfloat16)
            if is_direct(f):
                for i in DIRECT:
                    grad_direct(f, i).start()
                continue
            for i in range(4):
                grad_first(f, i).start()

    def forward_grad(c):
        for f in parts_of(c):
            if is_direct(f):
                continue
            if PARTS[f][2] == "x":
                grad_first_wait(f, 0)
                for i in range(1, 4):
                    grad_second(f, i).start()
            else:
                for i in range(1, 4):
                    grad_first_wait(f, i)
                    grad_second(f, i).start()

    def project(c):
        for f in parts_of(c):
            if is_direct(f):
                for i in DIRECT:
                    grad_direct_wait(f, i)
                continue
            if PARTS[f][2] == "x":
                for i in range(1, 4):
                    grad_first_wait(f, i)
            else:
                grad_first_wait(f, 0)
            for i in range(1, 4):
                grad_second_wait(f, i)
        start, rows = span_of(c)
        tile = min(256, features)
        for n in range(features // tile):
            columns = pl.ds(n * tile, tile)
            value = jnp.dot(
                grad[:, :, :, pl.ds(start, rows)].reshape(total.shape[0], rows),
                hid[pl.ds(start, rows), columns],
                preferred_element_type=jnp.float32,
            )
            if c == 0:
                total[:, columns] = value
            else:
                total[:, columns] += value
            if c == len(CHUNKS) - 1:
                out_copy(n).start()

    def span_of(c):
        parts = CHUNKS[c][1]
        return parts[0][0], parts[-1][0] + parts[-1][1] - parts[0][0]

    def out_copy(n):
        tile = min(256, features)
        span = (pl.ds(0, total.shape[0]), pl.ds(n * tile, tile))
        return pltpu.make_async_copy(total.at[span], out_ref.at[span], io_sem.at[3 + n])

    def arrive(c):
        for k in CHUNKS[c][0]:
            sibling(k).wait_recv()

    def following_of(half):
        span = rows_all // 2
        rows = foll[pl.ds(half * span, span), :].astype(jnp.float32).T
        return jnp.where(core == 0, rows[:width], rows[width:])

    arrive(0)
    start_first(0)
    gather(2, 0).wait_recv()
    gather(4, 0).start()
    gather(1, 1).wait_recv()
    gather(4, 1).start()
    gather(2, 1).wait_recv()
    sibling(2).start()
    gather(1, 0).wait_recv()
    sibling(1).start()
    for p in range(2):
        gather(3, p).wait_recv()
        gather(6, p).start()
        gather(5, p).start()
    sibling(3).start()
    start_second(0)
    arrive(1)
    start_first(1)
    for k in range(1, 8):
        foll_exchange(k).start()
    for p in range(2):
        gather(4, p).wait_recv()
    sibling(4).start()
    gather(6, 0).wait_recv()
    gather(7, 0).start()
    gather(5, 1).wait_recv()
    gather(7, 1).start()
    gather(6, 1).wait_recv()
    sibling(6).start()
    gather(5, 0).wait_recv()
    sibling(5).start()
    arrive(2)
    start_first(2)
    start_second(1)
    foll_copy.wait()
    foll_sibling(0).start()
    for k in range(1, 8):
        foll_exchange(k).wait_recv()
        foll_sibling(k).start()
    for p in range(2):
        gather(7, p).wait_recv()
    sibling(7).start()
    for k in range(8):
        foll_sibling(k).wait_recv()
    for h in range(2):
        following[:, pl.ds(h * (rows_all // 2), rows_all // 2)] = following_of(h)
    start_grad(0)
    arrive(3)
    start_first(3)
    start_grad(1)
    start_second(2)
    forward_grad(0)
    start_second(3)
    forward_grad(1)
    start_grad(2)
    start_grad(3)
    forward_grad(2)
    forward_grad(3)
    for c in range(len(CHUNKS)):
        project(c)

    for k in range(1, 8):
        for p in range(2):
            gather(k, p).wait_send()
    for k in range(8):
        sibling(k).wait_send()
    for k in range(8):
        if k:
            foll_exchange(k).wait_send()
        foll_sibling(k).wait_send()
    for f in range(len(PARTS)):
        if is_direct(f):
            for i in DIRECT:
                sum_direct(f, i).wait_send()
                grad_direct(f, i).wait_send()
            continue
        for i in peers(f, 0):
            sum_first(f, i).wait_send()
        for i in peers(f, 1):
            sum_second(f, i).wait_send()
        for i in range(4):
            grad_first(f, i).wait_send()
        for i in range(1, 4):
            grad_second(f, i).wait_send()
    for n in range(features // min(256, features)):
        out_copy(n).wait()


def gradient(used, foll, w_flat, n_tp):
    block, features = used.shape
    outs = w_flat.shape[0]
    width = outs // n_tp
    rows = 16 * block
    parts = len(PARTS)
    any_spec = pl.BlockSpec(memory_space=pl.ANY)
    dma = pltpu.SemaphoreType.DMA
    return pl.pallas_call(
        gradient_kernel,
        out_shape=jax.ShapeDtypeStruct((outs, features), jnp.float32),
        in_specs=[any_spec] * 3,
        out_specs=any_spec,
        scratch_shapes=[
            pltpu.VMEM((rows, features), jnp.bfloat16),
            pltpu.VMEM((outs, features), jnp.bfloat16),
            pltpu.VMEM((rows, 128), jnp.bfloat16),
            pltpu.VMEM((width, rows), jnp.float32),
            pltpu.VMEM((2, 4, width, rows), jnp.bfloat16),
            pltpu.VMEM((3, 2, width, rows), jnp.bfloat16),
            pltpu.VMEM((4, width, rows), jnp.bfloat16),
            pltpu.VMEM((4, width, rows), jnp.bfloat16),
            pltpu.VMEM((width, rows), jnp.float32),
            pltpu.VMEM((4, width, rows), jnp.bfloat16),
            pltpu.VMEM((7, width, rows), jnp.bfloat16),
            pltpu.VMEM((2, 4, width, rows), jnp.bfloat16),
            pltpu.VMEM((outs, features), jnp.float32),
            dma((7,)), dma((8, 2)), dma((8, 2)), dma((8,)), dma((8,)), dma((16,)), dma((16,)),
            dma((parts, 4)), dma((parts, 4)), dma((parts, 4)), dma((parts, 4)),
            dma((parts, 4)), dma((parts, 4)), dma((parts, 4)), dma((parts, 4)),
            dma((parts, 8)), dma((parts, 8)), dma((parts, 8)), dma((parts, 8)),
        ],
        compiler_params=pltpu.CompilerParams(
            collective_id=0, has_side_effects=True, vmem_limit_bytes=58 * 2**20
        ),
        name="gradient",
    )(used, foll, w_flat)


WRITES = 8


def write_kernel(in_ref, out_ref, buf, sem):
    rows = in_ref.shape[0] // WRITES

    def piece(n, out):
        span = pl.ds(n * rows, rows)
        if out:
            return pltpu.make_async_copy(buf.at[span], out_ref.at[span], sem.at[1, n])
        return pltpu.make_async_copy(in_ref.at[span], buf.at[span], sem.at[0, n])

    for n in range(WRITES):
        piece(n, False).start()
    for n in range(WRITES):
        piece(n, False).wait()
        piece(n, True).start()
    for n in range(WRITES):
        piece(n, True).wait()


def write(grad):
    any_spec = pl.BlockSpec(memory_space=pl.ANY)
    return pl.pallas_call(
        write_kernel,
        out_shape=jax.ShapeDtypeStruct(grad.shape, grad.dtype),
        in_specs=[any_spec],
        out_specs=any_spec,
        scratch_shapes=[pltpu.VMEM(grad.shape, grad.dtype), pltpu.SemaphoreType.DMA((2, WRITES))],
        compiler_params=pltpu.CompilerParams(vmem_limit_bytes=58 * 2**20),
        name="write",
    )(grad)


def shards(query, k_cache, v_cache, ctx_len, residual, accepted, w_draft):
    requests, new_tokens, heads, head_dim = query.shape
    slots = k_cache.shape[2]
    hidden, used, foll = attention(
        query.reshape(requests, new_tokens * heads, head_dim),
        k_cache.reshape(requests, slots, head_dim),
        v_cache.reshape(requests, slots, head_dim),
        ctx_len, residual, accepted,
    )
    features, groups, width = w_draft.shape
    w_flat = w_draft.transpose(1, 2, 0).reshape(groups * width, features)
    grad = write(gradient(used, foll, w_flat, groups))
    return hidden, grad.reshape(groups, width, features).transpose(2, 0, 1)


def solution(mesh):
    placed = (
        P("req", None, "tp", None),
        P("req", "tp", None, None),
        P("req", "tp", None, None),
        P("req"),
        P("req", "tp"),
        P(),
        P("tp", None, "req"),
    )
    return jax.shard_map(
        shards,
        mesh=mesh,
        in_specs=placed,
        out_specs=(P("req", "tp"), P("tp", None, "req")),
        check_vma=False,
    )
```
